512 devices in a mesh: sub: 64 (over x, z_hi, y), shot: 8 (over z_lo, core).
Axes of the slice: x: 4, y: 8, z: 8 (z_hi: 2, z_lo: 4; z = z_hi * 4 + z_lo), core: 2. Of those that a mesh axis runs over, the one named last changes fastest.
Arguments:
- adjoint_source: float32 [8, 2, 64, 16, 8, 256], P('shot', None, 'sub'), may hold values from -6 to 6
- forward_field: float32 [8, 2, 64, 16, 8, 256], P('shot', None, 'sub'), may hold values from -6 to 6
- kappa: float32 [64, 16, 8, 256], P('sub'), may hold values from 1 to 4
- damping: float32 [64, 16, 8, 256], P('sub'), may hold values from 0.1 to 1
Outputs:
- adjoint_field: float32 [8, 2, 64, 16, 8, 256], P('shot', None, 'sub')
- gradient: float32 [64, 16, 8, 256], P('sub', 'shot')
The draws below stay inside these ranges and needn't reach their ends.
All inputs are finite; a program needn't handle non-finite values.
Results may differ from the reference program's by a relative error of at most 0.00007.
Values sent between devices are 32-bit elements; how exact they have to be, the bound alone decides.
No kernel may reach another device: no remote copies, remote signals or barrier semaphores. Data moves between devices by JAX's collectives and lax.ppermute only.
A program may use at most 64 MiB of HBM per device.

```python
import math
import jax
import jax.numpy as jnp
from jax import lax

CX = 16
CY = 8
CZ = 256
SWEEPS = 4
PX = 4
PY = 4
PZ = 4
SUBS = 64
SHOTS = 8
NX = 64
NY = 32
NZ = 1024


def block_scale(key, shape, shards, least, top_value):
    factor_of = 1.0
    for dim, shards_of in shards:
        heights = jax.random.uniform(jax.random.fold_in(jax.random.fold_in(key, 6), dim), (shards_of,), jnp.float32, least / len(shards), top_value / len(shards))
        factor_of = factor_of * jnp.repeat(jnp.exp(heights), shape[dim] // shards_of).reshape((-1,) + (1,) * (len(shape) - 1 - dim))
    return factor_of


def bell_draw(key, shape, scale, bound, cuts=(), dtype=jnp.bfloat16):
    factor_of = block_scale(key, shape, cuts, -0.22, 0.18) if cuts else 1.0
    array = jax.random.normal(key, shape, jnp.float32) * scale * factor_of
    return jnp.minimum(jnp.maximum(array, -bound), bound).astype(dtype)


def setup_inputs(seed: int = 0) -> dict:
    key_list = jax.random.split(jax.random.key(seed), 5)
    adjoint_source = bell_draw(key_list[0], (SHOTS, 2, SUBS, CX, CY, CZ), 1.0, 6.0, ((0, 8), (2, 64)), jnp.float32)
    forward_field = bell_draw(key_list[1], (SHOTS, 2, SUBS, CX, CY, CZ), 1.0, 6.0, ((0, 8), (2, 64)), jnp.float32)
    kappa = jnp.clip(1.0 + 3.0 * jax.random.uniform(key_list[2], (SUBS, CX, CY, CZ), jnp.float32) ** block_scale(key_list[2], (SUBS, CX, CY, CZ), ((0, 64),), -0.2, 0.2), 1.0, 4.0)
    damping = jnp.clip(jnp.exp(math.log(1.0) - 2.3025851 * jax.random.uniform(key_list[3], (SUBS, CX, CY, CZ), jnp.float32) ** block_scale(key_list[3], (SUBS, CX, CY, CZ), ((0, 64),), -0.2, 0.2)), 0.1, 1.0)
    return {"adjoint_source": adjoint_source, "forward_field": forward_field, "kappa": kappa, "damping": damping}


A_COEF = 2.0 ** (2.0 / 3.0)
B_COEF = 2.0 ** (-4.0 / 3.0)
CENTER = 13.5
RELAX = 0.7


def through(values, dimension):
    length = values.shape[dimension]
    middle = lax.slice_in_dim(values, 1, length - 1, axis=dimension)
    lower = lax.slice_in_dim(values, 0, length - 2, axis=dimension)
    upper = lax.slice_in_dim(values, 2, length, axis=dimension)
    return A_COEF * middle + B_COEF * (lower + upper)


def padded(values, dimension):
    widths = [(0, 0)] * values.ndim
    widths[dimension] = (1, 1)
    return through(jnp.pad(values, widths), dimension)


def smooth(values):
    for offset in range(3):
        values = padded(values, values.ndim - 3 + offset)
    return values


def cmul(diag_re, diag_im, values):
    real_part = values[:, 0]
    imag_part = values[:, 1]
    return jnp.stack([diag_re * real_part - diag_im * imag_part, diag_re * imag_part + diag_im * real_part], axis=1)


def cscale(scale_re, scale_im, values):
    shaped = (-1,) + (1,) * (values.ndim - 2)
    return cmul(scale_re.reshape(shaped), scale_im.reshape(shaped), values)


def inner(left, right):
    dims = tuple(range(1, left.ndim - 1))
    real_part = jnp.sum(left[:, 0] * right[:, 0] + left[:, 1] * right[:, 1], axis=dims)
    imag_part = jnp.sum(left[:, 0] * right[:, 1] - left[:, 1] * right[:, 0], axis=dims)
    return real_part, imag_part


def squares(values):
    dims = tuple(range(1, values.ndim - 1))
    return jnp.sum(values[:, 0] * values[:, 0] + values[:, 1] * values[:, 1], axis=dims)


def to_grid(blocked):
    leading = blocked.shape[:-4]
    count = len(leading)
    shaped = blocked.reshape(leading + (PZ, PY, PX, CX, CY, CZ))
    order = tuple(range(count)) + (count + 2, count + 3, count + 1, count + 4, count + 0, count + 5)
    return jnp.transpose(shaped, order).reshape(leading + (NX, NY, NZ))


def from_grid(grid):
    leading = grid.shape[:-3]
    count = len(leading)
    shaped = grid.reshape(leading + (PX, CX, PY, CY, PZ, CZ))
    order = tuple(range(count)) + (count + 4, count + 2, count + 0, count + 1, count + 3, count + 5)
    return jnp.transpose(shaped, order).reshape(leading + (SUBS, CX, CY, CZ))


def blocks(grid):
    widths = [(0, 0)] * (grid.ndim - 3) + [(1, 1)] * 3
    framed = jnp.pad(grid, widths)
    pieces = []
    for third in range(PZ):
        for second in range(PY):
            for first in range(PX):
                pieces.append(framed[..., first * CX:first * CX + CX + 2, second * CY:second * CY + CY + 2, third * CZ:third * CZ + CZ + 2])
    return jnp.stack(pieces, axis=grid.ndim - 3)


def reference(adjoint_source, forward_field, kappa, damping):
    kappa_grid = to_grid(kappa)
    damping_grid = to_grid(damping)
    diag_re = CENTER - kappa_grid
    diag_im = kappa_grid * damping_grid
    pivot_re = diag_re - A_COEF ** 3
    modulus = pivot_re * pivot_re + diag_im * diag_im
    inv_re = pivot_re / modulus
    inv_im = -diag_im / modulus
    framed = blocks(jnp.stack([diag_re, diag_im, inv_re, inv_im]))

    def operate(field):
        return cmul(diag_re, diag_im, field) - smooth(field)

    def precondition(resid):
        extended = blocks(resid)
        approx = RELAX * cmul(framed[2], framed[3], extended)
        for sweep in range(SWEEPS - 1):
            defect = extended - (cmul(framed[0], framed[1], approx) - smooth(approx))
            approx = approx + RELAX * cmul(framed[2], framed[3], defect)
        return to_grid(approx[..., 1:-1, 1:-1, 1:-1])

    def solve_shot(pair):
        source, forward = pair
        start = to_grid(source)[None]
        first_dir = precondition(start)
        first_img = operate(first_dir)
        norm_one = squares(first_img)
        proj_re, proj_im = inner(first_img, start)
        alpha_re = proj_re / norm_one
        alpha_im = proj_im / norm_one
        solution = cscale(alpha_re, alpha_im, first_dir)
        resid = start - cscale(alpha_re, alpha_im, first_img)
        second_dir = precondition(resid)
        second_img = operate(second_dir)
        cross_re, cross_im = inner(first_img, second_img)
        gamma_re = cross_re / norm_one
        gamma_im = cross_im / norm_one
        new_dir = second_dir - cscale(gamma_re, gamma_im, first_dir)
        new_img = second_img - cscale(gamma_re, gamma_im, first_img)
        norm_two = squares(new_img)
        next_re, next_im = inner(new_img, resid)
        solution = solution + cscale(next_re / norm_two, next_im / norm_two, new_dir)
        wave = to_grid(forward)
        adjoint = solution[0]
        real_prod = wave[0] * adjoint[0] + wave[1] * adjoint[1]
        imag_prod = wave[1] * adjoint[0] - wave[0] * adjoint[1]
        return from_grid(adjoint), real_prod - damping_grid * imag_prod

    adjoint_field, terms = lax.map(solve_shot, (adjoint_source, forward_field))
    gradient = from_grid(jnp.sum(terms, axis=0))
    return adjoint_field, gradient
```

```python
import jax
import jax.numpy as jnp
from jax import lax
from jax.sharding import PartitionSpec as P

SWEEPS = 4
PX = 4


A_COEF = 2.0 ** (2.0 / 3.0)
B_COEF = 2.0 ** (-4.0 / 3.0)
CENTER = 13.5
RELAX = 0.7


def passed_along(x, axis, by):
    devices = lax.axis_size(axis)
    pairs = [(i, i + by) for i in range(devices) if 0 <= i + by < devices]
    return lax.ppermute(x, axis, pairs)


def through(values, dimension):
    length = values.shape[dimension]
    middle = lax.slice_in_dim(values, 1, length - 1, axis=dimension)
    lower = lax.slice_in_dim(values, 0, length - 2, axis=dimension)
    upper = lax.slice_in_dim(values, 2, length, axis=dimension)
    return A_COEF * middle + B_COEF * (lower + upper)


def padded(values, dimension):
    widths = [(0, 0)] * values.ndim
    widths[dimension] = (1, 1)
    return through(jnp.pad(values, widths), dimension)


def smooth(values):
    for offset in range(3):
        values = padded(values, values.ndim - 3 + offset)
    return values


def cmul(diag_re, diag_im, values):
    real_part = values[:, 0]
    imag_part = values[:, 1]
    return jnp.stack(
        [diag_re * real_part - diag_im * imag_part, diag_re * imag_part + diag_im * real_part],
        axis=1,
    )


def cscale(scale_re, scale_im, values):
    shaped = (-1,) + (1,) * (values.ndim - 2)
    return cmul(scale_re.reshape(shaped), scale_im.reshape(shaped), values)


def inner(left, right):
    dims = tuple(range(1, left.ndim - 1))
    real_part = jnp.sum(left[:, 0] * right[:, 0] + left[:, 1] * right[:, 1], axis=dims)
    imag_part = jnp.sum(left[:, 0] * right[:, 1] - left[:, 1] * right[:, 0], axis=dims)
    return (real_part, imag_part)


def squares(values):
    dims = tuple(range(1, values.ndim - 1))
    return jnp.sum(values[:, 0] * values[:, 0] + values[:, 1] * values[:, 1], axis=dims)


def neighbours_of():
    devices = lax.axis_size("sub")
    across = min(4, devices // 16)
    deepest = devices // (PX * across)
    index = lax.axis_index("sub")
    first = index % PX
    second = index // PX % across
    third = index // (PX * across)
    return [
        (1, first > 0, first < PX - 1),
        (PX, second > 0, second < across - 1),
        (PX * across, third > 0, third < deepest - 1),
    ]


def extend(values, dimension, stride, has_lower, has_upper, depth):
    length = values.shape[dimension]
    top_face = lax.slice_in_dim(values, length - depth, length, axis=dimension)
    bottom_face = lax.slice_in_dim(values, 0, depth, axis=dimension)
    below = passed_along(top_face, "sub", stride)
    above = passed_along(bottom_face, "sub", -stride)
    below = jnp.where(has_lower, below, jnp.zeros_like(below))
    above = jnp.where(has_upper, above, jnp.zeros_like(above))
    return jnp.concatenate([below, values, above], axis=dimension)


def with_rim(values, depth):
    base = values.ndim - 3
    for offset, entry in enumerate(neighbours_of()):
        stride, has_lower, has_upper = entry
        values = extend(values, base + offset, stride, has_lower, has_upper, depth)
    return values


def inner_cells(values):
    return values[..., 1:-1, 1:-1, 1:-1]


def local(adjoint_source, forward_field, kappa, damping):
    local_kappa = kappa[0]
    local_damping = damping[0]
    diag_re = CENTER - local_kappa
    diag_im = local_kappa * local_damping
    pivot_re = diag_re - A_COEF**3
    modulus = pivot_re * pivot_re + diag_im * diag_im
    inv_re = pivot_re / modulus
    inv_im = -diag_im / modulus
    coefficients = jnp.stack([diag_re, diag_im, inv_re, inv_im])
    start = adjoint_source[:, :, 0]

    def sweeps(extended, framed):
        approx = RELAX * cmul(framed[2], framed[3], extended)
        for sweep in range(SWEEPS - 1):
            defect = extended - (cmul(framed[0], framed[1], approx) - smooth(approx))
            approx = approx + RELAX * cmul(framed[2], framed[3], defect)
        return inner_cells(approx)

    def operate(field):
        extended = with_rim(field, 1)
        base = extended.ndim - 3
        neighbours = through(through(through(extended, base), base + 1), base + 2)
        return cmul(diag_re, diag_im, field) - neighbours

    framed = with_rim(coefficients, 1)
    first_dir = sweeps(with_rim(start, 1), framed)
    first_wide = with_rim(first_dir, 2)
    base = first_wide.ndim - 3
    around = through(through(through(first_wide, base), base + 1), base + 2)
    first_ext = cmul(framed[0], framed[1], inner_cells(first_wide)) - around
    first_img = inner_cells(first_ext)
    second_dir = sweeps(first_ext, framed)
    second_img = operate(second_dir)

    norm_here = squares(first_img)
    proj_here = inner(first_img, start)
    cross_here = inner(first_img, second_img)
    safe = jnp.where(norm_here > 0, norm_here, 1.0)
    cross_here = (cross_here[0] / safe, cross_here[1] / safe)
    part = second_img - cscale(*cross_here, first_img)
    pair_here = inner(part, start)
    mine = jnp.stack([norm_here, *proj_here, *cross_here, squares(part), *pair_here])[:, 0]
    devices = lax.axis_size("sub")
    table = lax.all_to_all(jnp.broadcast_to(mine[None], (devices, 8)), "sub", 0, 0)
    norm, proj_re, proj_im, cross_re, cross_im, rest, pair_re, pair_im = [table[:, n] for n in range(8)]
    total = jnp.sum(norm)
    alpha_re = jnp.sum(proj_re) / total
    alpha_im = jnp.sum(proj_im) / total
    mean_re = jnp.sum(norm * cross_re) / total
    mean_im = jnp.sum(norm * cross_im) / total
    off_re = cross_re - mean_re
    off_im = cross_im - mean_im
    size = jnp.sum(rest + norm * (off_re * off_re + off_im * off_im))
    beta_re = jnp.sum(pair_re + off_re * proj_re + off_im * proj_im) / size
    beta_im = jnp.sum(pair_im + off_re * proj_im - off_im * proj_re) / size
    lead_re = alpha_re - (beta_re * mean_re - beta_im * mean_im)
    lead_im = alpha_im - (beta_re * mean_im + beta_im * mean_re)
    solution = cscale(lead_re, lead_im, first_dir) + cscale(beta_re, beta_im, second_dir)

    wave = forward_field[:, :, 0]
    real_prod = wave[:, 0] * solution[:, 0] + wave[:, 1] * solution[:, 1]
    imag_prod = wave[:, 1] * solution[:, 0] - wave[:, 0] * solution[:, 1]
    partial_terms = jnp.sum(real_prod - local_damping * imag_prod, axis=0)
    shots = lax.axis_size("shot")
    rows = partial_terms.shape[0] // shots
    shares = partial_terms.reshape((shots, rows) + partial_terms.shape[1:])
    share = jnp.sum(lax.all_to_all(shares, "shot", 0, 0), axis=0)
    return (solution[:, :, None], share[None])


def solution(mesh):
    return jax.shard_map(
        local,
        mesh=mesh,
        in_specs=(
            P("shot", None, "sub", None, None, None),
            P("shot", None, "sub", None, None, None),
            P("sub", None, None, None),
            P("sub", None, None, None),
        ),
        out_specs=(P("shot", None, "sub", None, None, None), P("sub", "shot", None, None)),
        check_vma=False,
    )
```

```python
import jax
import jax.numpy as jnp
from jax import lax
from jax.experimental import pallas as pl
from jax.experimental.pallas import tpu as pltpu
from jax.sharding import PartitionSpec as P

SWEEPS = 4
PX = 4
PY = 4
PZ = 4
CX = 16
CY = 8
CZ = 256
CENTER = 13.5
RELAX = 0.7

SCALE = 16.0
MIDDLE = 4.0
PIVOT = 64.0

GROUP = PX * PY
SLAB = CZ // GROUP
DEEP = 8
THICK = SLAB + 2 * DEEP
LANES = 128
TILE = 8

PLANES = CX + 4
SLOT = CY + 3
SLOTS = 6
TILES = 9
BASE = 8
ROWS = BASE + TILES * TILE + 8
BODY = slice(BASE, BASE + TILES * TILE)
WIDE = 40
OWN = 11
FIELDS = 4
STATS = 8
BACK = FIELDS * SLAB + STATS
UNROLL = 3
VMEM_LIMIT = 48 * 1024 * 1024


def slot_of(unit):
    i, j = unit % PX, unit // PX
    if i < PX - 1:
        return j, i
    return (PX, j) if j < PY - 1 else (PX + 1, 0)


def first_row(slot):
    return BASE + SLOT * slot


def lanes_of(values):
    return lax.broadcasted_iota(jnp.int32, values.shape, values.ndim - 1)


def turn_kernel(source_ref, kappa_ref, damping_ref, own_ref, low_ref, high_ref):
    for field in range(FIELDS):
        for tile in range(CZ // LANES):
            here = slice(tile * LANES, (tile + 1) * LANES)
            if field < 2:
                values = source_ref[field, :, :, here]
            else:
                values = (kappa_ref, damping_ref)[field - 2][:, :, here]
            own_ref[field, here] = values.reshape(LANES, LANES).T
        low_ref[field] = own_ref[field, 0:DEEP]
        high_ref[field] = own_ref[field, CZ - DEEP:CZ]


def message_kernel(own_ref, below_ref, above_ref, out_ref):
    for field in range(FIELDS):
        for target in range(GROUP):
            first = target * SLAB - DEEP
            low = max(first, 0)
            high = min(first + THICK, CZ)
            out_ref[target, field, low - first:high - first] = own_ref[field, low:high]
        out_ref[0, field, 0:DEEP] = below_ref[field]
        out_ref[GROUP - 1, field, THICK - DEEP:THICK] = above_ref[field]


def total(values):
    return jnp.sum(jnp.sum(values, axis=0, keepdims=True), axis=1, keepdims=True)


def solve_kernel(got_ref, back_ref, r_ref, w_ref, d_ref, z_ref, y_ref, q_ref, u_ref, turn_ref, turned_ref):
    place = lax.rem(lax.axis_index("sub"), GROUP)
    is_first = place == 0
    is_last = place == GROUP - 1
    low_at = jnp.where(is_first, 0, 3)
    high_at = jnp.where(is_last, 30, 27)

    turn_ref[...] = jnp.zeros_like(turn_ref)
    for ref in (r_ref, w_ref, d_ref):
        @pl.loop(0, PLANES)
        def _(plane):
            for part in range(2):
                ref[part, plane] = jnp.zeros((ROWS, LANES), jnp.float32)
    for ref in (z_ref, y_ref):
        for part in range(2):
            ref[part, :, 0:BASE] = jnp.zeros((PLANES, BASE, LANES), jnp.float32)
            ref[part, :, ROWS - 8:ROWS] = jnp.zeros((PLANES, 8, LANES), jnp.float32)
    for part in range(2):
        for plane in (0, PLANES - 1):
            u_ref[part, plane] = jnp.zeros((ROWS, LANES), jnp.float32)
        for plane in (1, PLANES - 2):
            q_ref[part, plane] = jnp.zeros((ROWS, LANES), jnp.float32)

    for unit in range(GROUP):
        slot, group = slot_of(unit)
        at = group * WIDE
        for field in range(FIELDS):
            turn_ref[slot, field, pl.ds(at + low_at, DEEP)] = got_ref[unit, field, 0:DEEP]
            turn_ref[slot, field, at + OWN:at + OWN + SLAB] = got_ref[unit, field, DEEP:DEEP + SLAB]
            turn_ref[slot, field, pl.ds(at + high_at, DEEP)] = got_ref[unit, field, DEEP + SLAB:THICK]

    def fix(targets):
        for unit in range(GROUP):
            slot, group = slot_of(unit)
            at = group * WIDE
            for field in range(FIELDS):
                for target, source in targets:
                    if source is None:
                        row = jnp.zeros((1, LANES), jnp.float32)
                    else:
                        row = got_ref[unit, field, source:source + 1]
                    turn_ref[slot, field, at + target:at + target + 1] = row

    @pl.when(is_first)
    def _():
        fix(((8, DEEP), (9, None), (10, DEEP - 1)))

    @pl.when(is_last)
    def _():
        fix(((27, DEEP + SLAB), (28, None), (29, DEEP + SLAB - 1)))

    for slot in range(SLOTS):
        for field in range(FIELDS):
            turned_ref[slot, field] = turn_ref[slot, field].T

    @pl.loop(0, CX)
    def _(plane):
        at = pl.ds(pl.multiple_of(plane * TILE, TILE), TILE)
        for slot in range(SLOTS):
            b_re, b_im, kappa, damping = [turned_ref[slot, field, at] for field in range(FIELDS)]
            rows = slice(first_row(slot) + 1, first_row(slot) + 1 + CY)
            d_re = CENTER - kappa
            d_im = kappa * damping
            p_re = d_re - MIDDLE
            factor = jnp.where(kappa > 0, (RELAX / SCALE) / (p_re * p_re + d_im * d_im), 0.0)
            r_ref[0, 2 + plane, rows] = SCALE * b_re
            r_ref[1, 2 + plane, rows] = SCALE * b_im
            w_ref[0, 2 + plane, rows] = factor * p_re
            w_ref[1, 2 + plane, rows] = -factor * d_im
            d_ref[0, 2 + plane, rows] = SCALE * d_re
            d_ref[1, 2 + plane, rows] = SCALE * d_im

    def swap_ends(ref):
        def run(pairs):
            @pl.loop(2, 2 + CX)
            def _(plane):
                for part in range(2):
                    values = ref[part, plane, BODY]
                    lane = lax.rem(lanes_of(values), WIDE)
                    up = pltpu.roll(values, 3, 1)
                    down = pltpu.roll(values, LANES - 3, 1)
                    (a, b) = pairs
                    ref[part, plane, BODY] = jnp.where(lane == a, down, jnp.where(lane == b, up, values))

        @pl.when(is_first)
        def _():
            run((8, 10))

        @pl.when(is_last)
        def _():
            run((27, 29))

    def swap_sides(ref):
        one = jnp.zeros((TILE, LANES), jnp.float32)
        lane = lanes_of(one)
        last, first = CX + 1, 2

        def rows(slot):
            return slice(first_row(slot) + 1, first_row(slot) + 1 + CY)

        for part in range(2):
            for j in range(PY):
                here = rows(j)
                moved_up = pltpu.roll(ref[part, last, here], WIDE, 1)
                ref[part, 1, here] = jnp.where((lane >= WIDE) & (lane < 3 * WIDE), moved_up, ref[part, 1, here])
                slot, group = slot_of(PX - 1 + PX * j)
                end = rows(slot)
                inside = (lane >= group * WIDE) & (lane < (group + 1) * WIDE)
                shift = (2 - group) * WIDE
                moved_down = pltpu.roll(ref[part, first, here], LANES - WIDE, 1)
                from_end = pltpu.roll(ref[part, first, end], shift, 1) if shift else ref[part, first, end]
                ref[part, PLANES - 2, here] = jnp.where(
                    lane < 2 * WIDE, moved_down, jnp.where(lane < 3 * WIDE, from_end, ref[part, PLANES - 2, here]))
                to_end = ref[part, last, here]
                to_end = pltpu.roll(to_end, LANES - shift, 1) if shift else to_end
                ref[part, 1, end] = jnp.where(inside, to_end, ref[part, 1, end])

        def across(plane):
            for part in range(2):
                def row(slot, n):
                    return slice(first_row(slot) + n, first_row(slot) + n + 1)

                for j in range(PY):
                    if j > 0:
                        ref[part, plane, row(j, 0)] = ref[part, plane, row(j - 1, CY)]
                    if j < PY - 1:
                        ref[part, plane, row(j, CY + 1)] = ref[part, plane, row(j + 1, 1)]
                top = ref[part, plane, row(4, CY)]
                bottom = ref[part, plane, row(4, 1)]
                extra = ref[part, plane, row(5, 1)]
                lane = lanes_of(top)
                old = ref[part, plane, row(4, 0)]
                ref[part, plane, row(4, 0)] = jnp.where(
                    (lane >= WIDE) & (lane < 3 * WIDE), pltpu.roll(top, WIDE, 1), old)
                old = ref[part, plane, row(4, CY + 1)]
                ref[part, plane, row(4, CY + 1)] = jnp.where(
                    lane < 2 * WIDE, pltpu.roll(bottom, LANES - WIDE, 1),
                    jnp.where(lane < 3 * WIDE, pltpu.roll(extra, 2 * WIDE, 1), old))
                old = ref[part, plane, row(5, 0)]
                ref[part, plane, row(5, 0)] = jnp.where(lane < WIDE, pltpu.roll(top, LANES - 2 * WIDE, 1), old)

        loop(1, PLANES - 1, across)

    def loop(first, last, body):
        def step(plane, carry):
            body(plane)
            return carry

        lax.fori_loop(first, last, step, 0, unroll=UNROLL)

    swap_sides(r_ref)
    swap_sides(w_ref)

    def mix(ref, plane):
        for part in range(2):
            for t in range(TILES):
                at = BASE + t * TILE
                here = ref[part, plane, at:at + TILE]
                mixed = ref[part, plane, at - 1:at + TILE - 1] + ref[part, plane, at + 1:at + TILE + 1] + MIDDLE * here
                u_ref[part, plane, at:at + TILE] = (
                    pltpu.roll(mixed, 1, 1) + pltpu.roll(mixed, LANES - 1, 1) + MIDDLE * mixed)

    def smoothed(part, plane, at):
        return u_ref[part, plane - 1, at] + u_ref[part, plane + 1, at] + MIDDLE * u_ref[part, plane, at]

    def tiles():
        return [slice(BASE + t * TILE, BASE + (t + 1) * TILE) for t in range(TILES)]

    def sweep(ref, first, last, body):
        for plane in range(1, first + 2):
            mix(ref, plane)

        def step(plane):
            body(plane)
            mix(ref, plane + 2)

        loop(first, PLANES - 3, step)
        for plane in range(PLANES - 3, last + 1):
            body(plane)

    def precondition(ref, right_ref):
        def start(plane):
            for at in tiles():
                r_re, r_im = right_ref[0, plane, at], right_ref[1, plane, at]
                w_re, w_im = w_ref[0, plane, at], w_ref[1, plane, at]
                ref[0, plane, at] = w_re * r_re - w_im * r_im
                ref[1, plane, at] = w_re * r_im + w_im * r_re

        def update(plane):
            for at in tiles():
                z_re, z_im = ref[0, plane, at], ref[1, plane, at]
                w_re, w_im = w_ref[0, plane, at], w_ref[1, plane, at]
                g_re = (right_ref[0, plane, at] + smoothed(0, plane, at)) - PIVOT * z_re
                g_im = (right_ref[1, plane, at] + smoothed(1, plane, at)) - PIVOT * z_im
                ref[0, plane, at] = (1.0 - RELAX) * z_re + (w_re * g_re - w_im * g_im)
                ref[1, plane, at] = (1.0 - RELAX) * z_im + (w_re * g_im + w_im * g_re)

        loop(1, PLANES - 1, start)
        for number in range(1, SWEEPS):
            final = number == SWEEPS - 1
            sweep(ref, 2 if final else 1, PLANES - 3 if final else PLANES - 2, update)
        swap_ends(ref)
        swap_sides(ref)

    def image(ref, out_ref):
        def body(plane):
            for at in tiles():
                z_re, z_im = ref[0, plane, at], ref[1, plane, at]
                d_re, d_im = d_ref[0, plane, at], d_ref[1, plane, at]
                out_ref[0, plane, at] = (d_re * z_re - d_im * z_im) - smoothed(0, plane, at)
                out_ref[1, plane, at] = (d_re * z_im + d_im * z_re) - smoothed(1, plane, at)

        sweep(ref, 2, PLANES - 3, body)

    precondition(z_ref, r_ref)
    image(z_ref, q_ref)
    swap_ends(q_ref)
    swap_sides(q_ref)
    precondition(y_ref, q_ref)
    image(y_ref, w_ref)

    def own_cells(t):
        shape = (TILE, LANES)
        row = lax.broadcasted_iota(jnp.int32, shape, 0) + t * TILE
        lane = lax.broadcasted_iota(jnp.int32, shape, 1)
        y = lax.rem(row, SLOT)
        z = lax.rem(lane, WIDE)
        inside = (y >= 1) & (y <= CY) & (z >= OWN) & (z < OWN + SLAB)
        return inside & ((row < 5 * SLOT) & (lane < 3 * WIDE) | (row < SLOTS * SLOT) & (lane < WIDE))

    zero = jnp.zeros((TILE, LANES), jnp.float32)

    def first_sums(plane, sums):
        norm, proj_re, proj_im, cross_re, cross_im = sums
        for t, at in enumerate(tiles()):
            keep = own_cells(t)
            q_re = jnp.where(keep, q_ref[0, plane, at], 0.0)
            q_im = jnp.where(keep, q_ref[1, plane, at], 0.0)
            b_re, b_im = r_ref[0, plane, at], r_ref[1, plane, at]
            t_re, t_im = w_ref[0, plane, at], w_ref[1, plane, at]
            norm = norm + (q_re * q_re + q_im * q_im)
            proj_re = proj_re + (q_re * b_re + q_im * b_im)
            proj_im = proj_im + (q_re * b_im - q_im * b_re)
            cross_re = cross_re + (q_re * t_re + q_im * t_im)
            cross_im = cross_im + (q_re * t_im - q_im * t_re)
        return norm, proj_re, proj_im, cross_re, cross_im

    sums = lax.fori_loop(2, 2 + CX, first_sums, (zero,) * 5, unroll=2)
    norm, proj_re, proj_im, cross_re, cross_im = [total(v) for v in sums]
    safe = jnp.where(norm > 0, norm, 1.0)
    cross_re = cross_re / safe
    cross_im = cross_im / safe

    def second_sums(plane, sums):
        rest, pair_re, pair_im = sums
        for t, at in enumerate(tiles()):
            keep = own_cells(t)
            q_re, q_im = q_ref[0, plane, at], q_ref[1, plane, at]
            b_re, b_im = r_ref[0, plane, at], r_ref[1, plane, at]
            p_re = jnp.where(keep, w_ref[0, plane, at] - (cross_re * q_re - cross_im * q_im), 0.0)
            p_im = jnp.where(keep, w_ref[1, plane, at] - (cross_re * q_im + cross_im * q_re), 0.0)
            rest = rest + (p_re * p_re + p_im * p_im)
            pair_re = pair_re + (p_re * b_re + p_im * b_im)
            pair_im = pair_im + (p_re * b_im - p_im * b_re)
        return rest, pair_re, pair_im

    rest, pair_re, pair_im = [total(v) for v in lax.fori_loop(2, 2 + CX, second_sums, (zero,) * 3, unroll=2)]
    row = lax.broadcasted_iota(jnp.int32, (STATS, LANES), 0)
    table = jnp.zeros((STATS, LANES), jnp.float32)
    for n, value in enumerate((norm, proj_re, proj_im, cross_re, cross_im, rest, pair_re, pair_im)):
        table = jnp.where(row == n, value, table)

    for unit in range(GROUP):
        back_ref[unit, FIELDS * SLAB:BACK] = table
    for field in range(FIELDS):
        ref, part = (z_ref, y_ref)[field // 2], field % 2
        for slot in range(SLOTS):
            rows = slice(first_row(slot) + 1, first_row(slot) + 1 + CY)
            turned = ref[part, 2:2 + CX, rows].reshape(LANES, LANES).T
            for unit in range(GROUP):
                if slot_of(unit)[0] == slot:
                    at = slot_of(unit)[1] * WIDE + OWN
                    back_ref[unit, field * SLAB:(field + 1) * SLAB] = turned[at:at + SLAB]


def merged(rows):
    norm, proj_re, proj_im, cross_re, cross_im, rest, pair_re, pair_im = rows

    def over(values):
        return jnp.sum(values, axis=0, keepdims=True)

    whole = over(norm)
    mean_re = over(norm * cross_re) / whole
    mean_im = over(norm * cross_im) / whole
    off_re = cross_re - mean_re
    off_im = cross_im - mean_im
    return (whole, over(proj_re), over(proj_im), mean_re, mean_im,
            over(rest + norm * (off_re * off_re + off_im * off_im)),
            over(pair_re + off_re * proj_re + off_im * proj_im),
            over(pair_im + off_re * proj_im - off_im * proj_re))


def merge_kernel(back_ref, out_ref):
    rows = [back_ref[:, FIELDS * SLAB + n] for n in range(STATS)]
    for n, value in enumerate(merged(rows)):
        for target in range(PZ):
            out_ref[target, n:n + 1] = value


def finish_kernel(table_ref, back_ref, wave_ref, damping_ref, solution_ref, shares_ref):
    norm, proj_re, proj_im, mean_re, mean_im, size, pair_re, pair_im = merged([table_ref[:, n] for n in range(STATS)])
    beta_re = pair_re / size
    beta_im = pair_im / size
    lead_re = proj_re / norm - (beta_re * mean_re - beta_im * mean_im)
    lead_im = proj_im / norm - (beta_re * mean_im + beta_im * mean_re)
    shape = (SLAB, LANES)
    beta_re, beta_im, lead_re, lead_im = [jnp.broadcast_to(v, shape) for v in (beta_re, beta_im, lead_re, lead_im)]
    per = LANES // SLAB
    for tile in range(CZ // LANES):
        pieces = [[], []]
        for source in range(tile * per, (tile + 1) * per):
            f_re, f_im, s_re, s_im = [back_ref[source, n * SLAB:(n + 1) * SLAB] for n in range(FIELDS)]
            pieces[0].append((lead_re * f_re - lead_im * f_im) + (beta_re * s_re - beta_im * s_im))
            pieces[1].append((lead_re * f_im + lead_im * f_re) + (beta_re * s_im + beta_im * s_re))
        here = slice(tile * LANES, (tile + 1) * LANES)
        x_re, x_im = [jnp.concatenate(p, axis=0).T.reshape(CX, CY, LANES) for p in pieces]
        solution_ref[0, :, :, here] = x_re
        solution_ref[1, :, :, here] = x_im
        u_re, u_im = wave_ref[0, :, :, here], wave_ref[1, :, :, here]
        shares_ref[:, :, here] = (u_re * x_re + u_im * x_im) - damping_ref[:, :, here] * (u_im * x_re - u_re * x_im)


def moved(values, stride):
    steps = PX * PY * PZ
    pairs = []
    for index in range(steps):
        place = index // abs(stride) % 4 + (1 if stride > 0 else -1)
        if 0 <= place < 4:
            pairs.append((index, index + stride))
    return lax.ppermute(values, "sub", pairs)


def call(kernel, out_shapes, scratch=()):
    one = pl.BlockSpec(memory_space=pltpu.VMEM)

    def run(*args):
        return pl.pallas_call(
            kernel,
            out_shape=[jax.ShapeDtypeStruct(shape, jnp.float32) for shape in out_shapes],
            in_specs=[one] * len(args),
            out_specs=[one] * len(out_shapes),
            scratch_shapes=list(scratch),
            compiler_params=pltpu.CompilerParams(vmem_limit_bytes=VMEM_LIMIT),
        )(*args)

    return run


def local(adjoint_source, forward_field, kappa, damping):
    source = adjoint_source[0, :, 0]
    wave = forward_field[0, :, 0]
    kappa = kappa[0]
    damping = damping[0]
    face = (FIELDS, DEEP, LANES)
    own, low, high = call(turn_kernel, [(FIELDS, CZ, LANES), face, face])(source, kappa, damping)
    below = moved(high, PX * PY)
    above = moved(low, -PX * PY)
    message, = call(message_kernel, [(GROUP, FIELDS, THICK, LANES)])(own, below, above)
    layers = [[k * GROUP + n for n in range(GROUP)] for k in range(PZ)]
    columns = [[k * GROUP + n for k in range(PZ)] for n in range(GROUP)]
    got = lax.all_to_all(message, "sub", 0, 0, axis_index_groups=layers)
    work = pltpu.VMEM((2, PLANES, ROWS, LANES), jnp.float32)
    turn = pltpu.VMEM((SLOTS, FIELDS, LANES, LANES), jnp.float32)
    back, = call(solve_kernel, [(GROUP, BACK, LANES)], [work] * 7 + [turn] * 2)(got)
    back = lax.all_to_all(back, "sub", 0, 0, axis_index_groups=layers)
    part, = call(merge_kernel, [(PZ, STATS, LANES)])(back)
    table = lax.all_to_all(part, "sub", 0, 0, axis_index_groups=columns)
    solved, shares = call(finish_kernel, [(2, CX, CY, CZ), (CX, CY, CZ)])(table, back, wave, damping)
    shots = lax.axis_size("shot")
    shares = shares.reshape(shots, CX // shots, CY, CZ)
    share = jnp.sum(lax.all_to_all(shares, "shot", 0, 0), axis=0)
    return (solved[None, :, None], share[None])


def solution(mesh):
    return jax.shard_map(
        local,
        mesh=mesh,
        in_specs=(
            P("shot", None, "sub", None, None, None),
            P("shot", None, "sub", None, None, None),
            P("sub", None, None, None),
            P("sub", None, None, None),
        ),
        out_specs=(P("shot", None, "sub", None, None, None), P("sub", "shot", None, None)),
        check_vma=False,
    )
```

```python
import jax
import jax.numpy as jnp
from jax import lax
from jax.experimental import pallas as pl
from jax.experimental.pallas import tpu as pltpu
from jax.sharding import PartitionSpec as P

SWEEPS = 4
PX = 4
PY = 4
PZ = 4
CX = 16
CY = 8
CZ = 256
CENTER = 13.5
RELAX = 0.7

SCALE = 16.0
MIDDLE = 4.0
PIVOT = 64.0

GROUP = PX * PY
SLAB = CZ // GROUP
RING = GROUP // 2
DEEP = 8
LANES = 128
TILE = 8

PLANES = CX + 4
SLOT = CY + 3
SLOTS = 6
TILES = 9
BASE = 8
ROWS = BASE + TILES * TILE + 8
BODY = slice(BASE, BASE + TILES * TILE)
WIDE = 40
OWN = 11
FIELDS = 4
STATS = 8
BACK = FIELDS * SLAB + STATS
VMEM_LIMIT = 24 * 1024 * 1024


def slot_of(unit):
    i, j = unit % PX, unit // PX
    if i < PX - 1:
        return j, i
    return (PX, j) if j < PY - 1 else (PX + 1, 0)


def first_row(slot):
    return BASE + SLOT * slot


def lanes_of(values):
    return lax.broadcasted_iota(jnp.int32, values.shape, values.ndim - 1)


def turn_kernel(source_ref, kappa_ref, damping_ref, out_ref, source_held, kappa_held, damping_held, turned_ref, sems):
    copies = [pltpu.make_async_copy(source_ref.at[0], source_held.at[0], sems.at[0]),
              pltpu.make_async_copy(source_ref.at[1], source_held.at[1], sems.at[1]),
              pltpu.make_async_copy(kappa_ref, kappa_held, sems.at[2]),
              pltpu.make_async_copy(damping_ref, damping_held, sems.at[3])]
    for copy in copies:
        copy.start()
    odd, turn = path()
    for field in range(FIELDS):
        copies[field].wait()
        held = (source_held.at[0], source_held.at[1], kappa_held, damping_held)[field]
        for tile in range(CZ // LANES):
            here = slice(tile * LANES, (tile + 1) * LANES)
            turned_ref[field, here] = held[:, :, here].reshape(LANES, LANES).T
    for device in range(GROUP):
        rows = pl.ds(pl.multiple_of(slab_of(device, odd, turn) * SLAB, SLAB), SLAB)
        for field in range(FIELDS):
            out_ref[device, field] = turned_ref[field, rows]


def edges_kernel(got_ref, low_ref, high_ref):
    low_ref[...] = got_ref[:, :, 0:DEEP]
    high_ref[...] = got_ref[:, :, SLAB - DEEP:SLAB]


def total(values):
    return jnp.sum(jnp.sum(values, axis=0, keepdims=True), axis=1, keepdims=True)


def path():
    return lax.rem(lax.axis_index("sub") // GROUP, 2), lax.axis_index("shot")


def slab_of(device, odd, turn):
    half, y = (divmod(device, RING) if isinstance(device, int) else (device // RING, lax.rem(device, RING)))
    there = lax.rem(y - turn - 1 + 2 * RING, RING)
    back = RING + lax.rem(turn - y + 2 * RING, RING)
    return jnp.where(half == odd, there, back)


def device_of(slab, odd, turn):
    if slab < RING:
        return odd * RING + lax.rem(turn + 1 + slab, RING)
    return (1 - odd) * RING + lax.rem(turn - slab + 3 * RING, RING)


def position():
    odd, turn = path()
    place = slab_of(lax.rem(lax.axis_index("sub"), GROUP), odd, turn)
    return place == 0, place == GROUP - 1


class Steps:

    def __init__(self, u_ref, w_ref, d_ref):
        self.is_first, self.is_last = position()
        self.u_ref, self.w_ref, self.d_ref = u_ref, w_ref, d_ref
        for part in range(2):
            for plane in (0, PLANES - 1):
                u_ref[part, plane] = jnp.zeros((ROWS, LANES), jnp.float32)

    def swap_ends(self, ref):
        def run(a, b):
            for plane in range(2, 2 + CX):
                for part in range(2):
                    for at in tiles():
                        values = ref[part, plane, at]
                        lane = lax.rem(lanes_of(values), WIDE)
                        up = pltpu.roll(values, 3, 1)
                        down = pltpu.roll(values, LANES - 3, 1)
                        ref[part, plane, at] = jnp.where(lane == a, down, jnp.where(lane == b, up, values))

        @pl.when(self.is_first)
        def _():
            run(8, 10)

        @pl.when(self.is_last)
        def _():
            run(27, 29)

    def swap_sides(self, ref):
        one = jnp.zeros((TILE, LANES), jnp.float32)
        lane = lanes_of(one)
        last, first = CX + 1, 2

        def rows(slot):
            return slice(first_row(slot) + 1, first_row(slot) + 1 + CY)

        for part in range(2):
            for j in range(PY):
                here = rows(j)
                moved_up = pltpu.roll(ref[part, last, here], WIDE, 1)
                ref[part, 1, here] = jnp.where((lane >= WIDE) & (lane < 3 * WIDE), moved_up, ref[part, 1, here])
                slot, group = slot_of(PX - 1 + PX * j)
                end = rows(slot)
                inside = (lane >= group * WIDE) & (lane < (group + 1) * WIDE)
                shift = (2 - group) * WIDE
                moved_down = pltpu.roll(ref[part, first, here], LANES - WIDE, 1)
                from_end = pltpu.roll(ref[part, first, end], shift, 1) if shift else ref[part, first, end]
                ref[part, PLANES - 2, here] = jnp.where(
                    lane < 2 * WIDE, moved_down, jnp.where(lane < 3 * WIDE, from_end, ref[part, PLANES - 2, here]))
                to_end = ref[part, last, here]
                to_end = pltpu.roll(to_end, LANES - shift, 1) if shift else to_end
                ref[part, 1, end] = jnp.where(inside, to_end, ref[part, 1, end])

        def across(plane):
            for part in range(2):
                def row(slot, n):
                    return slice(first_row(slot) + n, first_row(slot) + n + 1)

                for j in range(PY):
                    if j > 0:
                        ref[part, plane, row(j, 0)] = ref[part, plane, row(j - 1, CY)]
                    if j < PY - 1:
                        ref[part, plane, row(j, CY + 1)] = ref[part, plane, row(j + 1, 1)]
                top = ref[part, plane, row(4, CY)]
                bottom = ref[part, plane, row(4, 1)]
                extra = ref[part, plane, row(5, 1)]
                lane = lanes_of(top)
                old = ref[part, plane, row(4, 0)]
                ref[part, plane, row(4, 0)] = jnp.where(
                    (lane >= WIDE) & (lane < 3 * WIDE), pltpu.roll(top, WIDE, 1), old)
                old = ref[part, plane, row(4, CY + 1)]
                ref[part, plane, row(4, CY + 1)] = jnp.where(
                    lane < 2 * WIDE, pltpu.roll(bottom, LANES - WIDE, 1),
                    jnp.where(lane < 3 * WIDE, pltpu.roll(extra, 2 * WIDE, 1), old))
                old = ref[part, plane, row(5, 0)]
                ref[part, plane, row(5, 0)] = jnp.where(lane < WIDE, pltpu.roll(top, LANES - 2 * WIDE, 1), old)

        for plane in range(1, PLANES - 1):
            across(plane)

    def mix(self, ref, plane):
        for part in range(2):
            for t in range(TILES):
                at = BASE + t * TILE
                here = ref[part, plane, at:at + TILE]
                mixed = ref[part, plane, at - 1:at + TILE - 1] + ref[part, plane, at + 1:at + TILE + 1] + MIDDLE * here
                self.u_ref[part, plane, at:at + TILE] = (
                    pltpu.roll(mixed, 1, 1) + pltpu.roll(mixed, LANES - 1, 1) + MIDDLE * mixed)

    def smoothed(self, part, plane, at):
        u_ref = self.u_ref
        return u_ref[part, plane - 1, at] + u_ref[part, plane + 1, at] + MIDDLE * u_ref[part, plane, at]

    def sweep(self, ref, first, last, body):
        for plane in range(1, first + 2):
            self.mix(ref, plane)
        for plane in range(first, last + 1):
            body(plane)
            if plane + 2 < PLANES - 1:
                self.mix(ref, plane + 2)

    def precondition(self, ref, right_ref):
        w_ref = self.w_ref
        for part in range(2):
            ref[part, :, 0:BASE] = jnp.zeros((PLANES, BASE, LANES), jnp.float32)
            ref[part, :, ROWS - 8:ROWS] = jnp.zeros((PLANES, 8, LANES), jnp.float32)

        def start(plane):
            for at in tiles():
                r_re, r_im = right_ref[0, plane, at], right_ref[1, plane, at]
                w_re, w_im = w_ref[0, plane, at], w_ref[1, plane, at]
                ref[0, plane, at] = w_re * r_re - w_im * r_im
                ref[1, plane, at] = w_re * r_im + w_im * r_re

        def update(plane):
            for at in tiles():
                z_re, z_im = ref[0, plane, at], ref[1, plane, at]
                w_re, w_im = w_ref[0, plane, at], w_ref[1, plane, at]
                g_re = (right_ref[0, plane, at] + self.smoothed(0, plane, at)) - PIVOT * z_re
                g_im = (right_ref[1, plane, at] + self.smoothed(1, plane, at)) - PIVOT * z_im
                ref[0, plane, at] = (1.0 - RELAX) * z_re + (w_re * g_re - w_im * g_im)
                ref[1, plane, at] = (1.0 - RELAX) * z_im + (w_re * g_im + w_im * g_re)

        for plane in range(1, PLANES - 1):
            start(plane)

        @pl.loop(0, SWEEPS - 1)
        def _(number):
            self.sweep(ref, 1, PLANES - 2, update)

        self.swap_ends(ref)
        self.swap_sides(ref)

    def image(self, ref, out_ref):
        d_ref = self.d_ref

        def body(plane):
            for at in tiles():
                z_re, z_im = ref[0, plane, at], ref[1, plane, at]
                d_re, d_im = d_ref[0, plane, at], d_ref[1, plane, at]
                out_ref[0, plane, at] = (d_re * z_re - d_im * z_im) - self.smoothed(0, plane, at)
                out_ref[1, plane, at] = (d_re * z_im + d_im * z_re) - self.smoothed(1, plane, at)

        self.sweep(ref, 2, PLANES - 3, body)


def tiles():
    return [slice(BASE + t * TILE, BASE + (t + 1) * TILE) for t in range(TILES)]


def send_back(ref, back_ref, first):
    for part in range(2):
        for slot in range(SLOTS):
            rows = slice(first_row(slot) + 1, first_row(slot) + 1 + CY)
            turned = ref[part, 2:2 + CX, rows].reshape(LANES, LANES).T
            for unit in range(GROUP):
                if slot_of(unit)[0] == slot:
                    at = slot_of(unit)[1] * WIDE + OWN
                    back_ref[unit, first + part * SLAB:first + (part + 1) * SLAB] = turned[at:at + SLAB]


def solve_kernel(got_ref, below_ref, above_ref, back_ref, r_ref, w_ref, d_ref, q_ref, z_ref, u_ref, turn_ref, turned_ref):
    is_first, is_last = position()
    low_at = jnp.where(is_first, 0, 3)
    high_at = jnp.where(is_last, 30, 27)

    turn_ref[...] = jnp.zeros_like(turn_ref)
    for ref in (r_ref, w_ref, d_ref):
        for plane in range(1, PLANES - 1):
            for part in range(2):
                ref[part, plane, BODY] = jnp.zeros((TILES * TILE, LANES), jnp.float32)
    for part in range(2):
        for plane in (1, PLANES - 2):
            q_ref[part, plane] = jnp.zeros((ROWS, LANES), jnp.float32)

    for unit in range(GROUP):
        slot, group = slot_of(unit)
        at = group * WIDE
        for field in range(FIELDS):
            turn_ref[slot, field, pl.ds(at + low_at, DEEP)] = below_ref[unit, field]
            turn_ref[slot, field, at + OWN:at + OWN + SLAB] = got_ref[unit, field]
            turn_ref[slot, field, pl.ds(at + high_at, DEEP)] = above_ref[unit, field]

    def fix(targets):
        for unit in range(GROUP):
            slot, group = slot_of(unit)
            at = group * WIDE
            for field in range(FIELDS):
                for target, ref, source in targets:
                    if ref is None:
                        row = jnp.zeros((1, LANES), jnp.float32)
                    else:
                        row = ref[unit, field, source:source + 1]
                    turn_ref[slot, field, at + target:at + target + 1] = row

    @pl.when(is_first)
    def _():
        fix(((8, got_ref, 0), (9, None, 0), (10, below_ref, DEEP - 1)))

    @pl.when(is_last)
    def _():
        fix(((27, above_ref, 0), (28, None, 0), (29, got_ref, SLAB - 1)))

    for slot in range(SLOTS):
        for field in range(FIELDS):
            turned_ref[slot, field] = turn_ref[slot, field].T

    def fill(plane, carry):
        at = pl.ds(pl.multiple_of(plane * TILE, TILE), TILE)
        for slot in range(SLOTS):
            b_re, b_im, kappa, damping = [turned_ref[slot, field, at] for field in range(FIELDS)]
            rows = slice(first_row(slot) + 1, first_row(slot) + 1 + CY)
            d_re = CENTER - kappa
            d_im = kappa * damping
            p_re = d_re - MIDDLE
            factor = jnp.where(kappa > 0, (RELAX / SCALE) / (p_re * p_re + d_im * d_im), 0.0)
            r_ref[0, 2 + plane, rows] = SCALE * b_re
            r_ref[1, 2 + plane, rows] = SCALE * b_im
            w_ref[0, 2 + plane, rows] = factor * p_re
            w_ref[1, 2 + plane, rows] = -factor * d_im
            d_ref[0, 2 + plane, rows] = SCALE * d_re
            d_ref[1, 2 + plane, rows] = SCALE * d_im
        return carry

    lax.fori_loop(0, CX, fill, 0, unroll=4)

    steps = Steps(u_ref, w_ref, d_ref)
    steps.swap_sides(r_ref)
    steps.swap_sides(w_ref)
    steps.precondition(z_ref, r_ref)
    send_back(z_ref, back_ref, 0)
    steps.image(z_ref, q_ref)
    steps.swap_ends(q_ref)
    steps.swap_sides(q_ref)
    steps.precondition(z_ref, q_ref)
    send_back(z_ref, back_ref, 2 * SLAB)
    steps.image(z_ref, w_ref)

    def own_cells(t):
        shape = (TILE, LANES)
        row = lax.broadcasted_iota(jnp.int32, shape, 0) + t * TILE
        lane = lax.broadcasted_iota(jnp.int32, shape, 1)
        y = lax.rem(row, SLOT)
        z = lax.rem(lane, WIDE)
        inside = (y >= 1) & (y <= CY) & (z >= OWN) & (z < OWN + SLAB)
        return inside & ((row < 5 * SLOT) & (lane < 3 * WIDE) | (row < SLOTS * SLOT) & (lane < WIDE))

    zero = jnp.zeros((TILE, LANES), jnp.float32)

    def first_sums(plane, sums):
        norm, proj_re, proj_im, cross_re, cross_im = sums
        for t, at in enumerate(tiles()):
            keep = own_cells(t)
            q_re = jnp.where(keep, q_ref[0, plane, at], 0.0)
            q_im = jnp.where(keep, q_ref[1, plane, at], 0.0)
            b_re, b_im = r_ref[0, plane, at], r_ref[1, plane, at]
            t_re, t_im = w_ref[0, plane, at], w_ref[1, plane, at]
            norm = norm + (q_re * q_re + q_im * q_im)
            proj_re = proj_re + (q_re * b_re + q_im * b_im)
            proj_im = proj_im + (q_re * b_im - q_im * b_re)
            cross_re = cross_re + (q_re * t_re + q_im * t_im)
            cross_im = cross_im + (q_re * t_im - q_im * t_re)
        return norm, proj_re, proj_im, cross_re, cross_im

    sums = (zero,) * 5
    for plane in range(2, 2 + CX):
        sums = first_sums(plane, sums)
    norm, proj_re, proj_im, cross_re, cross_im = [total(v) for v in sums]
    safe = jnp.where(norm > 0, norm, 1.0)
    cross_re = cross_re / safe
    cross_im = cross_im / safe

    def second_sums(plane, sums):
        rest, pair_re, pair_im = sums
        for t, at in enumerate(tiles()):
            keep = own_cells(t)
            q_re, q_im = q_ref[0, plane, at], q_ref[1, plane, at]
            b_re, b_im = r_ref[0, plane, at], r_ref[1, plane, at]
            p_re = jnp.where(keep, w_ref[0, plane, at] - (cross_re * q_re - cross_im * q_im), 0.0)
            p_im = jnp.where(keep, w_ref[1, plane, at] - (cross_re * q_im + cross_im * q_re), 0.0)
            rest = rest + (p_re * p_re + p_im * p_im)
            pair_re = pair_re + (p_re * b_re + p_im * b_im)
            pair_im = pair_im + (p_re * b_im - p_im * b_re)
        return rest, pair_re, pair_im

    sums = (zero,) * 3
    for plane in range(2, 2 + CX):
        sums = second_sums(plane, sums)
    rest, pair_re, pair_im = [total(v) for v in sums]
    row = lax.broadcasted_iota(jnp.int32, (STATS, LANES), 0)
    table = jnp.zeros((STATS, LANES), jnp.float32)
    for n, value in enumerate((norm, proj_re, proj_im, cross_re, cross_im, rest, pair_re, pair_im)):
        table = jnp.where(row == n, value, table)

    for unit in range(GROUP):
        back_ref[unit, FIELDS * SLAB:BACK] = table


def merged(rows):
    norm, proj_re, proj_im, cross_re, cross_im, rest, pair_re, pair_im = rows

    def over(values):
        return jnp.sum(values, axis=0, keepdims=True)

    whole = over(norm)
    mean_re = over(norm * cross_re) / whole
    mean_im = over(norm * cross_im) / whole
    off_re = cross_re - mean_re
    off_im = cross_im - mean_im
    return (whole, over(proj_re), over(proj_im), mean_re, mean_im,
            over(rest + norm * (off_re * off_re + off_im * off_im)),
            over(pair_re + off_re * proj_re + off_im * proj_im),
            over(pair_im + off_re * proj_im - off_im * proj_re))


def merge_kernel(back_ref, out_ref):
    rows = [back_ref[:, FIELDS * SLAB + n] for n in range(STATS)]
    for n, value in enumerate(merged(rows)):
        for target in range(PZ):
            out_ref[target, n:n + 1] = value


def finish_kernel(table_ref, back_ref, wave_ref, damping_ref, solution_ref, shares_ref):
    norm, proj_re, proj_im, mean_re, mean_im, size, pair_re, pair_im = merged([table_ref[:, n] for n in range(STATS)])
    beta_re = pair_re / size
    beta_im = pair_im / size
    lead_re = proj_re / norm - (beta_re * mean_re - beta_im * mean_im)
    lead_im = proj_im / norm - (beta_re * mean_im + beta_im * mean_re)
    shape = (SLAB, LANES)
    beta_re, beta_im, lead_re, lead_im = [jnp.broadcast_to(v, shape) for v in (beta_re, beta_im, lead_re, lead_im)]
    per = LANES // SLAB
    odd, turn = path()
    for tile in range(CZ // LANES):
        pieces = [[], []]
        for source in range(tile * per, (tile + 1) * per):
            at = device_of(source, odd, turn)
            f_re, f_im, s_re, s_im = [back_ref[at, n * SLAB:(n + 1) * SLAB] for n in range(FIELDS)]
            pieces[0].append((lead_re * f_re - lead_im * f_im) + (beta_re * s_re - beta_im * s_im))
            pieces[1].append((lead_re * f_im + lead_im * f_re) + (beta_re * s_im + beta_im * s_re))
        here = slice(tile * LANES, (tile + 1) * LANES)
        x_re, x_im = [jnp.concatenate(p, axis=0).T.reshape(CX, CY, LANES) for p in pieces]
        solution_ref[0, :, :, here] = x_re
        solution_ref[1, :, :, here] = x_im
        u_re, u_im = wave_ref[0, :, :, here], wave_ref[1, :, :, here]
        shares_ref[:, :, here] = (u_re * x_re + u_im * x_im) - damping_ref[:, :, here] * (u_im * x_re - u_re * x_im)


def moved(values, step):
    shots = lax.axis_size("shot")
    pairs = []
    for turn in range(shots):
        chain = []
        for layer in range(PZ):
            odd = layer % 2
            for slab in range(GROUP):
                if slab < RING:
                    device = odd * RING + (turn + 1 + slab) % RING
                else:
                    device = (1 - odd) * RING + (turn - slab) % RING
                chain.append((layer * GROUP + device) * shots + turn)
        pairs += list(zip(chain, chain[1:]) if step > 0 else zip(chain[1:], chain))
    return lax.ppermute(values, ("sub", "shot"), pairs)


def call(kernel, out_shapes, scratch=(), space=pltpu.VMEM, limit=VMEM_LIMIT):
    one = pl.BlockSpec(memory_space=pltpu.VMEM)
    given = pl.BlockSpec(memory_space=space)

    def run(*args):
        return pl.pallas_call(
            kernel,
            out_shape=[jax.ShapeDtypeStruct(shape, jnp.float32) for shape in out_shapes],
            in_specs=[given] * len(args),
            out_specs=[one] * len(out_shapes),
            scratch_shapes=list(scratch),
            compiler_params=pltpu.CompilerParams(vmem_limit_bytes=limit),
        )(*args)

    return run


def local(adjoint_source, forward_field, kappa, damping):
    source = adjoint_source[0, :, 0]
    wave = forward_field[0, :, 0]
    kappa = kappa[0]
    damping = damping[0]
    block = (CX, CY, CZ)
    held = [pltpu.VMEM(shape, jnp.float32) for shape in ((2,) + block, block, block, (FIELDS, CZ, LANES))]
    message, = call(turn_kernel, [(GROUP, FIELDS, SLAB, LANES)], held + [pltpu.SemaphoreType.DMA((FIELDS,))],
                    pltpu.HBM, 60 * 1024 * 1024)(source, kappa, damping)
    layers = [[k * GROUP + n for n in range(GROUP)] for k in range(PZ)]
    columns = [[k * GROUP + n for k in range(PZ)] for n in range(GROUP)]
    got = lax.all_to_all(message, "sub", 0, 0, axis_index_groups=layers)
    edge = (GROUP, FIELDS, DEEP, LANES)
    low, high = call(edges_kernel, [edge, edge])(got)
    below = moved(high, 1)
    above = moved(low, -1)
    work = pltpu.VMEM((2, PLANES, ROWS, LANES), jnp.float32)
    turn = pltpu.VMEM((SLOTS, FIELDS, LANES, LANES), jnp.float32)
    back, = call(solve_kernel, [(GROUP, BACK, LANES)], [work] * 6 + [turn] * 2)(got, below, above)
    back = lax.all_to_all(back, "sub", 0, 0, axis_index_groups=layers)
    part, = call(merge_kernel, [(PZ, STATS, LANES)])(back)
    table = lax.all_to_all(part, "sub", 0, 0, axis_index_groups=columns)
    solved, shares = call(finish_kernel, [(2, CX, CY, CZ), (CX, CY, CZ)])(table, back, wave, damping)
    shots = lax.axis_size("shot")
    shares = shares.reshape(shots, CX // shots, CY, CZ)
    share = jnp.sum(lax.all_to_all(shares, "shot", 0, 0), axis=0)
    return (solved[None, :, None], share[None])


def solution(mesh):
    return jax.shard_map(
        local,
        mesh=mesh,
        in_specs=(
            P("shot", None, "sub", None, None, None),
            P("shot", None, "sub", None, None, None),
            P("sub", None, None, None),
            P("sub", None, None, None),
        ),
        out_specs=(P("shot", None, "sub", None, None, None), P("sub", "shot", None, None)),
        check_vma=False,
    )
```

```python
import jax
import jax.numpy as jnp
from jax import lax
from jax.experimental import pallas as pl
from jax.experimental.pallas import tpu as pltpu
from jax.sharding import PartitionSpec as P

SWEEPS = 4
PX = 4
PY = 4
PZ = 4
CX = 16
CY = 8
CZ = 256
CENTER = 13.5
RELAX = 0.7

SCALE = 16.0
MIDDLE = 4.0
PIVOT = 64.0

GROUP = PX * PY
SLAB = CZ // GROUP
RING = GROUP // 2
DEEP = 8
LANES = 128
TILE = 8

PLANES = CX + 4
SLOT = CY + 3
SLOTS = 6
TILES = 9
BASE = 8
ROWS = BASE + TILES * TILE + 8
BODY = slice(BASE, BASE + TILES * TILE)
WIDE = 40
OWN = 11
FIELDS = 4
STATS = 8
BACK = FIELDS * SLAB + STATS
VMEM_LIMIT = 24 * 1024 * 1024


def slot_of(unit):
    i, j = unit % PX, unit // PX
    if i < PX - 1:
        return j, i
    return (PX, j) if j < PY - 1 else (PX + 1, 0)


def first_row(slot):
    return BASE + SLOT * slot


def lanes_of(values):
    return lax.broadcasted_iota(jnp.int32, values.shape, values.ndim - 1)


def turn_kernel(source_ref, kappa_ref, damping_ref, out_ref, source_held, kappa_held, damping_held, turned_ref, sems):
    copies = [pltpu.make_async_copy(source_ref.at[0], source_held.at[0], sems.at[0]),
              pltpu.make_async_copy(source_ref.at[1], source_held.at[1], sems.at[1]),
              pltpu.make_async_copy(kappa_ref, kappa_held, sems.at[2]),
              pltpu.make_async_copy(damping_ref, damping_held, sems.at[3])]
    for copy in copies:
        copy.start()
    odd, turn = path()
    for field in range(FIELDS):
        copies[field].wait()
        held = (source_held.at[0], source_held.at[1], kappa_held, damping_held)[field]
        for tile in range(CZ // LANES):
            here = slice(tile * LANES, (tile + 1) * LANES)
            turned_ref[field, here] = held[:, :, here].reshape(LANES, LANES).T
    for device in range(GROUP):
        rows = pl.ds(pl.multiple_of(slab_of(device, odd, turn) * SLAB, SLAB), SLAB)
        for field in range(FIELDS):
            out_ref[device, field] = turned_ref[field, rows]


def edges_kernel(got_ref, low_ref, high_ref):
    low_ref[...] = got_ref[:, :, 0:DEEP]
    high_ref[...] = got_ref[:, :, SLAB - DEEP:SLAB]


def total(values):
    return jnp.sum(jnp.sum(values, axis=0, keepdims=True), axis=1, keepdims=True)


def path():
    return lax.rem(lax.axis_index("sub") // GROUP, 2), lax.axis_index("shot")


def slab_of(device, odd, turn):
    half, y = (divmod(device, RING) if isinstance(device, int) else (device // RING, lax.rem(device, RING)))
    there = lax.rem(y - turn - 1 + 2 * RING, RING)
    back = RING + lax.rem(turn - y + 2 * RING, RING)
    return jnp.where(half == odd, there, back)


def device_of(slab, odd, turn):
    if slab < RING:
        return odd * RING + lax.rem(turn + 1 + slab, RING)
    return (1 - odd) * RING + lax.rem(turn - slab + 3 * RING, RING)


def position():
    odd, turn = path()
    place = slab_of(lax.rem(lax.axis_index("sub"), GROUP), odd, turn)
    return place == 0, place == GROUP - 1


class Steps:

    def __init__(self, u_ref, w_ref, d_ref):
        self.is_first, self.is_last = position()
        self.u_ref, self.w_ref, self.d_ref = u_ref, w_ref, d_ref
        for part in range(2):
            for plane in (0, PLANES - 1):
                u_ref[part, plane] = jnp.zeros((ROWS, LANES), jnp.float32)

    def swap_ends(self, ref):
        def run(a, b):
            lane = lax.broadcasted_iota(jnp.int32, (TILE, LANES), 1)
            place = lax.rem(lane, WIDE)
            source = jnp.where(place == a, lane + 3, jnp.where(place == b, lane - 3, lane))
            source = jnp.minimum(source, LANES - 1)
            for plane in range(2, 2 + CX):
                for part in range(2):
                    for at in own_tiles():
                        ref[part, plane, at] = jnp.take_along_axis(ref[part, plane, at], source, axis=1)

        @pl.when(self.is_first)
        def _():
            run(8, 10)

        @pl.when(self.is_last)
        def _():
            run(27, 29)

    def swap_sides(self, ref):
        one = jnp.zeros((TILE, LANES), jnp.float32)
        lane = lanes_of(one)
        last, first = CX + 1, 2

        def rows(slot):
            return slice(first_row(slot) + 1, first_row(slot) + 1 + CY)

        for part in range(2):
            for j in range(PY):
                here = rows(j)
                moved_up = pltpu.roll(ref[part, last, here], WIDE, 1)
                ref[part, 1, here] = jnp.where((lane >= WIDE) & (lane < 3 * WIDE), moved_up, ref[part, 1, here])
                slot, group = slot_of(PX - 1 + PX * j)
                end = rows(slot)
                inside = (lane >= group * WIDE) & (lane < (group + 1) * WIDE)
                shift = (2 - group) * WIDE
                moved_down = pltpu.roll(ref[part, first, here], LANES - WIDE, 1)
                from_end = pltpu.roll(ref[part, first, end], shift, 1) if shift else ref[part, first, end]
                ref[part, PLANES - 2, here] = jnp.where(
                    lane < 2 * WIDE, moved_down, jnp.where(lane < 3 * WIDE, from_end, ref[part, PLANES - 2, here]))
                to_end = ref[part, last, here]
                to_end = pltpu.roll(to_end, LANES - shift, 1) if shift else to_end
                ref[part, 1, end] = jnp.where(inside, to_end, ref[part, 1, end])

        def across(plane):
            for part in range(2):
                def row(slot, n):
                    return slice(first_row(slot) + n, first_row(slot) + n + 1)

                for j in range(PY):
                    if j > 0:
                        ref[part, plane, row(j, 0)] = ref[part, plane, row(j - 1, CY)]
                    if j < PY - 1:
                        ref[part, plane, row(j, CY + 1)] = ref[part, plane, row(j + 1, 1)]
                top = ref[part, plane, row(4, CY)]
                bottom = ref[part, plane, row(4, 1)]
                extra = ref[part, plane, row(5, 1)]
                lane = lanes_of(top)
                old = ref[part, plane, row(4, 0)]
                ref[part, plane, row(4, 0)] = jnp.where(
                    (lane >= WIDE) & (lane < 3 * WIDE), pltpu.roll(top, WIDE, 1), old)
                old = ref[part, plane, row(4, CY + 1)]
                ref[part, plane, row(4, CY + 1)] = jnp.where(
                    lane < 2 * WIDE, pltpu.roll(bottom, LANES - WIDE, 1),
                    jnp.where(lane < 3 * WIDE, pltpu.roll(extra, 2 * WIDE, 1), old))
                old = ref[part, plane, row(5, 0)]
                ref[part, plane, row(5, 0)] = jnp.where(lane < WIDE, pltpu.roll(top, LANES - 2 * WIDE, 1), old)

        for plane in range(1, PLANES - 1):
            across(plane)

    def mix(self, ref, plane, rows):
        for part in range(2):
            for at in rows:
                below, above = slice(at.start - 1, at.stop - 1), slice(at.start + 1, at.stop + 1)
                mixed = ref[part, plane, below] + ref[part, plane, above] + MIDDLE * ref[part, plane, at]
                self.u_ref[part, plane, at] = (
                    pltpu.roll(mixed, 1, 1) + pltpu.roll(mixed, LANES - 1, 1) + MIDDLE * mixed)

    def smoothed(self, part, plane, at):
        u_ref = self.u_ref
        return u_ref[part, plane - 1, at] + u_ref[part, plane + 1, at] + MIDDLE * u_ref[part, plane, at]

    def sweep(self, ref, first, last, body, rows):
        for plane in range(1, first + 2):
            self.mix(ref, plane, rows)
        for plane in range(first, last + 1):
            body(plane, rows)
            if plane + 2 < PLANES - 1:
                self.mix(ref, plane + 2, rows)

    def precondition(self, ref, right_ref):
        w_ref = self.w_ref
        for part in range(2):
            ref[part, :, 0:BASE] = jnp.zeros((PLANES, BASE, LANES), jnp.float32)
            ref[part, :, ROWS - 8:ROWS] = jnp.zeros((PLANES, 8, LANES), jnp.float32)

        def start(plane):
            for at in tiles():
                r_re, r_im = right_ref[0, plane, at], right_ref[1, plane, at]
                w_re, w_im = w_ref[0, plane, at], w_ref[1, plane, at]
                ref[0, plane, at] = w_re * r_re - w_im * r_im
                ref[1, plane, at] = w_re * r_im + w_im * r_re

        def update(plane, rows):
            for at in rows:
                z_re, z_im = ref[0, plane, at], ref[1, plane, at]
                w_re, w_im = w_ref[0, plane, at], w_ref[1, plane, at]
                g_re = (right_ref[0, plane, at] + self.smoothed(0, plane, at)) - PIVOT * z_re
                g_im = (right_ref[1, plane, at] + self.smoothed(1, plane, at)) - PIVOT * z_im
                ref[0, plane, at] = (1.0 - RELAX) * z_re + (w_re * g_re - w_im * g_im)
                ref[1, plane, at] = (1.0 - RELAX) * z_im + (w_re * g_im + w_im * g_re)

        for plane in range(1, PLANES - 1):
            start(plane)

        @pl.loop(0, SWEEPS - 2)
        def _(number):
            self.sweep(ref, 1, PLANES - 2, update, tiles())

        self.sweep(ref, 2, PLANES - 3, update, own_tiles())
        self.swap_ends(ref)
        self.swap_sides(ref)

    def image(self, ref, out_ref):
        d_ref = self.d_ref

        def body(plane, rows):
            for at in rows:
                z_re, z_im = ref[0, plane, at], ref[1, plane, at]
                d_re, d_im = d_ref[0, plane, at], d_ref[1, plane, at]
                out_ref[0, plane, at] = (d_re * z_re - d_im * z_im) - self.smoothed(0, plane, at)
                out_ref[1, plane, at] = (d_re * z_im + d_im * z_re) - self.smoothed(1, plane, at)

        self.sweep(ref, 2, PLANES - 3, body, own_tiles())


def tiles():
    return [slice(BASE + t * TILE, BASE + (t + 1) * TILE) for t in range(TILES)]


def own_tiles():
    return [slice(first_row(slot) + 1, first_row(slot) + 1 + CY) for slot in range(SLOTS)]


def send_back(ref, back_ref, first):
    for part in range(2):
        for slot in range(SLOTS):
            rows = slice(first_row(slot) + 1, first_row(slot) + 1 + CY)
            turned = ref[part, 2:2 + CX, rows].reshape(LANES, LANES).T
            for unit in range(GROUP):
                if slot_of(unit)[0] == slot:
                    at = slot_of(unit)[1] * WIDE + OWN
                    back_ref[unit, first + part * SLAB:first + (part + 1) * SLAB] = turned[at:at + SLAB]


def solve_kernel(got_ref, below_ref, above_ref, back_ref, r_ref, w_ref, d_ref, q_ref, z_ref, u_ref, turn_ref, turned_ref):
    is_first, is_last = position()
    low_at = jnp.where(is_first, 0, 3)
    high_at = jnp.where(is_last, 30, 27)

    turn_ref[...] = jnp.zeros_like(turn_ref)
    for ref in (r_ref, w_ref, d_ref, q_ref):
        for plane in range(1, PLANES - 1):
            for part in range(2):
                ref[part, plane, BODY] = jnp.zeros((TILES * TILE, LANES), jnp.float32)

    for unit in range(GROUP):
        slot, group = slot_of(unit)
        at = group * WIDE
        for field in range(FIELDS):
            turn_ref[slot, field, pl.ds(at + low_at, DEEP)] = below_ref[unit, field]
            turn_ref[slot, field, at + OWN:at + OWN + SLAB] = got_ref[unit, field]
            turn_ref[slot, field, pl.ds(at + high_at, DEEP)] = above_ref[unit, field]

    def fix(targets):
        for unit in range(GROUP):
            slot, group = slot_of(unit)
            at = group * WIDE
            for field in range(FIELDS):
                for target, ref, source in targets:
                    if ref is None:
                        row = jnp.zeros((1, LANES), jnp.float32)
                    else:
                        row = ref[unit, field, source:source + 1]
                    turn_ref[slot, field, at + target:at + target + 1] = row

    @pl.when(is_first)
    def _():
        fix(((8, got_ref, 0), (9, None, 0), (10, below_ref, DEEP - 1)))

    @pl.when(is_last)
    def _():
        fix(((27, above_ref, 0), (28, None, 0), (29, got_ref, SLAB - 1)))

    for slot in range(SLOTS):
        for field in range(FIELDS):
            turned_ref[slot, field] = turn_ref[slot, field].T

    def fill(plane, carry):
        at = pl.ds(pl.multiple_of(plane * TILE, TILE), TILE)
        for slot in range(SLOTS):
            b_re, b_im, kappa, damping = [turned_ref[slot, field, at] for field in range(FIELDS)]
            rows = slice(first_row(slot) + 1, first_row(slot) + 1 + CY)
            d_re = CENTER - kappa
            d_im = kappa * damping
            p_re = d_re - MIDDLE
            factor = jnp.where(kappa > 0, (RELAX / SCALE) / (p_re * p_re + d_im * d_im), 0.0)
            r_ref[0, 2 + plane, rows] = SCALE * b_re
            r_ref[1, 2 + plane, rows] = SCALE * b_im
            w_ref[0, 2 + plane, rows] = factor * p_re
            w_ref[1, 2 + plane, rows] = -factor * d_im
            d_ref[0, 2 + plane, rows] = SCALE * d_re
            d_ref[1, 2 + plane, rows] = SCALE * d_im
        return carry

    lax.fori_loop(0, CX, fill, 0, unroll=4)

    steps = Steps(u_ref, w_ref, d_ref)
    steps.swap_sides(r_ref)
    steps.swap_sides(w_ref)
    steps.precondition(z_ref, r_ref)
    send_back(z_ref, back_ref, 0)
    steps.image(z_ref, q_ref)
    steps.swap_ends(q_ref)
    steps.swap_sides(q_ref)
    steps.precondition(z_ref, q_ref)
    send_back(z_ref, back_ref, 2 * SLAB)
    steps.image(z_ref, w_ref)

    lane = lax.broadcasted_iota(jnp.int32, (TILE, LANES), 1)
    place = lax.rem(lane, WIDE)
    in_slab = (place >= OWN) & (place < OWN + SLAB)

    def over_cells(terms, count):
        sums = [jnp.zeros((TILE, LANES), jnp.float32)] * count
        for slot, at in enumerate(own_tiles()):
            here = terms(2, at)
            for plane in range(3, 2 + CX):
                here = [a + b for a, b in zip(here, terms(plane, at))]
            keep = in_slab if slot < SLOTS - 1 else in_slab & (lane < WIDE)
            sums = [a + jnp.where(keep, b, 0.0) for a, b in zip(sums, here)]
        return [total(v) for v in sums]

    def first_terms(plane, at):
        q_re, q_im = q_ref[0, plane, at], q_ref[1, plane, at]
        b_re, b_im = r_ref[0, plane, at], r_ref[1, plane, at]
        t_re, t_im = w_ref[0, plane, at], w_ref[1, plane, at]
        return (q_re * q_re + q_im * q_im, q_re * b_re + q_im * b_im, q_re * b_im - q_im * b_re,
                q_re * t_re + q_im * t_im, q_re * t_im - q_im * t_re)

    norm, proj_re, proj_im, cross_re, cross_im = over_cells(first_terms, 5)
    safe = jnp.where(norm > 0, norm, 1.0)
    cross_re = cross_re / safe
    cross_im = cross_im / safe
    mean_re = jnp.broadcast_to(cross_re, (TILE, LANES))
    mean_im = jnp.broadcast_to(cross_im, (TILE, LANES))

    def second_terms(plane, at):
        q_re, q_im = q_ref[0, plane, at], q_ref[1, plane, at]
        b_re, b_im = r_ref[0, plane, at], r_ref[1, plane, at]
        p_re = w_ref[0, plane, at] - (mean_re * q_re - mean_im * q_im)
        p_im = w_ref[1, plane, at] - (mean_re * q_im + mean_im * q_re)
        return p_re * p_re + p_im * p_im, p_re * b_re + p_im * b_im, p_re * b_im - p_im * b_re

    rest, pair_re, pair_im = over_cells(second_terms, 3)
    row = lax.broadcasted_iota(jnp.int32, (STATS, LANES), 0)
    table = jnp.zeros((STATS, LANES), jnp.float32)
    for n, value in enumerate((norm, proj_re, proj_im, cross_re, cross_im, rest, pair_re, pair_im)):
        table = jnp.where(row == n, value, table)

    for unit in range(GROUP):
        back_ref[unit, FIELDS * SLAB:BACK] = table


def merged(rows):
    norm, proj_re, proj_im, cross_re, cross_im, rest, pair_re, pair_im = rows

    def over(values):
        return jnp.sum(values, axis=0, keepdims=True)

    whole = over(norm)
    mean_re = over(norm * cross_re) / whole
    mean_im = over(norm * cross_im) / whole
    off_re = cross_re - mean_re
    off_im = cross_im - mean_im
    return (whole, over(proj_re), over(proj_im), mean_re, mean_im,
            over(rest + norm * (off_re * off_re + off_im * off_im)),
            over(pair_re + off_re * proj_re + off_im * proj_im),
            over(pair_im + off_re * proj_im - off_im * proj_re))


def merge_kernel(back_ref, out_ref):
    rows = [back_ref[:, FIELDS * SLAB + n] for n in range(STATS)]
    for n, value in enumerate(merged(rows)):
        for target in range(PZ):
            out_ref[target, n:n + 1] = value


def finish_kernel(table_ref, back_ref, wave_ref, damping_ref, solution_ref, shares_ref):
    norm, proj_re, proj_im, mean_re, mean_im, size, pair_re, pair_im = merged([table_ref[:, n] for n in range(STATS)])
    beta_re = pair_re / size
    beta_im = pair_im / size
    lead_re = proj_re / norm - (beta_re * mean_re - beta_im * mean_im)
    lead_im = proj_im / norm - (beta_re * mean_im + beta_im * mean_re)
    shape = (SLAB, LANES)
    beta_re, beta_im, lead_re, lead_im = [jnp.broadcast_to(v, shape) for v in (beta_re, beta_im, lead_re, lead_im)]
    per = LANES // SLAB
    odd, turn = path()
    for tile in range(CZ // LANES):
        pieces = [[], []]
        for source in range(tile * per, (tile + 1) * per):
            at = device_of(source, odd, turn)
            f_re, f_im, s_re, s_im = [back_ref[at, n * SLAB:(n + 1) * SLAB] for n in range(FIELDS)]
            pieces[0].append((lead_re * f_re - lead_im * f_im) + (beta_re * s_re - beta_im * s_im))
            pieces[1].append((lead_re * f_im + lead_im * f_re) + (beta_re * s_im + beta_im * s_re))
        here = slice(tile * LANES, (tile + 1) * LANES)
        x_re, x_im = [jnp.concatenate(p, axis=0).T.reshape(CX, CY, LANES) for p in pieces]
        solution_ref[0, :, :, here] = x_re
        solution_ref[1, :, :, here] = x_im
        u_re, u_im = wave_ref[0, :, :, here], wave_ref[1, :, :, here]
        shares_ref[:, :, here] = (u_re * x_re + u_im * x_im) - damping_ref[:, :, here] * (u_im * x_re - u_re * x_im)


def moved(values, step):
    shots = lax.axis_size("shot")
    pairs = []
    for turn in range(shots):
        chain = []
        for layer in range(PZ):
            odd = layer % 2
            for slab in range(GROUP):
                if slab < RING:
                    device = odd * RING + (turn + 1 + slab) % RING
                else:
                    device = (1 - odd) * RING + (turn - slab) % RING
                chain.append((layer * GROUP + device) * shots + turn)
        pairs += list(zip(chain, chain[1:]) if step > 0 else zip(chain[1:], chain))
    return lax.ppermute(values, ("sub", "shot"), pairs)


def call(kernel, out_shapes, scratch=(), space=pltpu.VMEM, limit=VMEM_LIMIT):
    one = pl.BlockSpec(memory_space=pltpu.VMEM)
    given = pl.BlockSpec(memory_space=space)

    def run(*args):
        return pl.pallas_call(
            kernel,
            out_shape=[jax.ShapeDtypeStruct(shape, jnp.float32) for shape in out_shapes],
            in_specs=[given] * len(args),
            out_specs=[one] * len(out_shapes),
            scratch_shapes=list(scratch),
            compiler_params=pltpu.CompilerParams(vmem_limit_bytes=limit),
        )(*args)

    return run


def local(adjoint_source, forward_field, kappa, damping):
    source = adjoint_source[0, :, 0]
    wave = forward_field[0, :, 0]
    kappa = kappa[0]
    damping = damping[0]
    block = (CX, CY, CZ)
    held = [pltpu.VMEM(shape, jnp.float32) for shape in ((2,) + block, block, block, (FIELDS, CZ, LANES))]
    message, = call(turn_kernel, [(GROUP, FIELDS, SLAB, LANES)], held + [pltpu.SemaphoreType.DMA((FIELDS,))],
                    pltpu.HBM, 60 * 1024 * 1024)(source, kappa, damping)
    layers = [[k * GROUP + n for n in range(GROUP)] for k in range(PZ)]
    columns = [[k * GROUP + n for k in range(PZ)] for n in range(GROUP)]
    got = lax.all_to_all(message, "sub", 0, 0, axis_index_groups=layers)
    edge = (GROUP, FIELDS, DEEP, LANES)
    low, high = call(edges_kernel, [edge, edge])(got)
    below = moved(high, 1)
    above = moved(low, -1)
    work = pltpu.VMEM((2, PLANES, ROWS, LANES), jnp.float32)
    turn = pltpu.VMEM((SLOTS, FIELDS, LANES, LANES), jnp.float32)
    back, = call(solve_kernel, [(GROUP, BACK, LANES)], [work] * 6 + [turn] * 2)(got, below, above)
    back = lax.all_to_all(back, "sub", 0, 0, axis_index_groups=layers)
    part, = call(merge_kernel, [(PZ, STATS, LANES)])(back)
    table = lax.all_to_all(part, "sub", 0, 0, axis_index_groups=columns)
    solved, shares = call(finish_kernel, [(2, CX, CY, CZ), (CX, CY, CZ)])(table, back, wave, damping)
    shots = lax.axis_size("shot")
    shares = shares.reshape(shots, CX // shots, CY, CZ)
    share = jnp.sum(lax.all_to_all(shares, "shot", 0, 0), axis=0)
    return (solved[None, :, None], share[None])


def solution(mesh):
    return jax.shard_map(
        local,
        mesh=mesh,
        in_specs=(
            P("shot", None, "sub", None, None, None),
            P("shot", None, "sub", None, None, None),
            P("sub", None, None, None),
            P("sub", None, None, None),
        ),
        out_specs=(P("shot", None, "sub", None, None, None), P("sub", "shot", None, None)),
        check_vma=False,
    )
```

```python
import jax
import jax.numpy as jnp
from jax import lax
from jax.experimental import pallas as pl
from jax.experimental.pallas import tpu as pltpu
from jax.sharding import PartitionSpec as P

SWEEPS = 4
PX = 4
PY = 4
PZ = 4
CX = 16
CY = 8
CZ = 256
CENTER = 13.5
RELAX = 0.7

SCALE = 16.0
MIDDLE = 4.0
PIVOT = 64.0

GROUP = PX * PY
SLAB = CZ // GROUP
RING = GROUP // 2
DEEP = 8
LANES = 128
TILE = 8

PLANES = CX + 4
SLOT = CY + 3
SLOTS = 6
TILES = 9
BASE = 8
ROWS = BASE + TILES * TILE + 8
BODY = slice(BASE, BASE + TILES * TILE)
WIDE = 40
OWN = 11
FIELDS = 4
STATS = 8
BACK = FIELDS * SLAB + STATS
VMEM_LIMIT = 24 * 1024 * 1024


def slot_of(unit):
    i, j = unit % PX, unit // PX
    if i < PX - 1:
        return j, i
    return (PX, j) if j < PY - 1 else (PX + 1, 0)


def first_row(slot):
    return BASE + SLOT * slot


def lanes_of(values):
    return lax.broadcasted_iota(jnp.int32, values.shape, values.ndim - 1)


def turn_kernel(source_ref, kappa_ref, damping_ref, out_ref, source_held, kappa_held, damping_held, turned_ref, sems):
    copies = [pltpu.make_async_copy(source_ref.at[0], source_held.at[0], sems.at[0]),
              pltpu.make_async_copy(source_ref.at[1], source_held.at[1], sems.at[1]),
              pltpu.make_async_copy(kappa_ref, kappa_held, sems.at[2]),
              pltpu.make_async_copy(damping_ref, damping_held, sems.at[3])]
    for copy in copies:
        copy.start()
    odd, turn = path()
    for field in range(FIELDS):
        copies[field].wait()
        held = (source_held.at[0], source_held.at[1], kappa_held, damping_held)[field]
        for tile in range(CZ // LANES):
            here = slice(tile * LANES, (tile + 1) * LANES)
            turned_ref[field, here] = held[:, :, here].reshape(LANES, LANES).T
    for device in range(GROUP):
        rows = pl.ds(pl.multiple_of(slab_of(device, odd, turn) * SLAB, SLAB), SLAB)
        for field in range(FIELDS):
            out_ref[device, field] = turned_ref[field, rows]


def edges_kernel(got_ref, low_ref, high_ref):
    low_ref[...] = got_ref[:, :, 0:DEEP]
    high_ref[...] = got_ref[:, :, SLAB - DEEP:SLAB]


def total(values):
    return jnp.sum(jnp.sum(values, axis=0, keepdims=True), axis=1, keepdims=True)


def path():
    return lax.rem(lax.axis_index("sub") // GROUP, 2), lax.axis_index("shot")


def slab_of(device, odd, turn):
    half, y = (divmod(device, RING) if isinstance(device, int) else (device // RING, lax.rem(device, RING)))
    there = lax.rem(y - turn - 1 + 2 * RING, RING)
    back = RING + lax.rem(turn - y + 2 * RING, RING)
    return jnp.where(half == odd, there, back)


def device_of(slab, odd, turn):
    if slab < RING:
        return odd * RING + lax.rem(turn + 1 + slab, RING)
    return (1 - odd) * RING + lax.rem(turn - slab + 3 * RING, RING)


def position():
    odd, turn = path()
    place = slab_of(lax.rem(lax.axis_index("sub"), GROUP), odd, turn)
    return place == 0, place == GROUP - 1


class Steps:

    def __init__(self, u_ref, w_ref, d_ref):
        self.is_first, self.is_last = position()
        self.u_ref, self.w_ref, self.d_ref = u_ref, w_ref, d_ref
        for part in range(2):
            for plane in (0, PLANES - 1):
                u_ref[part, plane] = jnp.zeros((ROWS, LANES), jnp.float32)

    def swap_ends(self, ref):
        def run(a, b):
            lane = lax.broadcasted_iota(jnp.int32, (TILE, LANES), 1)
            place = lax.rem(lane, WIDE)
            source = jnp.where(place == a, lane + 3, jnp.where(place == b, lane - 3, lane))
            source = jnp.minimum(source, LANES - 1)
            for plane in range(2, 2 + CX):
                for part in range(2):
                    for at in own_tiles():
                        ref[part, plane, at] = jnp.take_along_axis(ref[part, plane, at], source, axis=1)

        @pl.when(self.is_first)
        def _():
            run(8, 10)

        @pl.when(self.is_last)
        def _():
            run(27, 29)

    def swap_sides(self, ref):
        one = jnp.zeros((TILE, LANES), jnp.float32)
        lane = lanes_of(one)
        last, first = CX + 1, 2

        def rows(slot):
            return slice(first_row(slot) + 1, first_row(slot) + 1 + CY)

        for part in range(2):
            for j in range(PY):
                here = rows(j)
                moved_up = pltpu.roll(ref[part, last, here], WIDE, 1)
                ref[part, 1, here] = jnp.where((lane >= WIDE) & (lane < 3 * WIDE), moved_up, ref[part, 1, here])
                slot, group = slot_of(PX - 1 + PX * j)
                end = rows(slot)
                inside = (lane >= group * WIDE) & (lane < (group + 1) * WIDE)
                shift = (2 - group) * WIDE
                moved_down = pltpu.roll(ref[part, first, here], LANES - WIDE, 1)
                from_end = pltpu.roll(ref[part, first, end], shift, 1) if shift else ref[part, first, end]
                ref[part, PLANES - 2, here] = jnp.where(
                    lane < 2 * WIDE, moved_down, jnp.where(lane < 3 * WIDE, from_end, ref[part, PLANES - 2, here]))
                to_end = ref[part, last, here]
                to_end = pltpu.roll(to_end, LANES - shift, 1) if shift else to_end
                ref[part, 1, end] = jnp.where(inside, to_end, ref[part, 1, end])

        def across(plane):
            for part in range(2):
                def row(slot, n):
                    return slice(first_row(slot) + n, first_row(slot) + n + 1)

                for j in range(PY):
                    if j > 0:
                        ref[part, plane, row(j, 0)] = ref[part, plane, row(j - 1, CY)]
                    if j < PY - 1:
                        ref[part, plane, row(j, CY + 1)] = ref[part, plane, row(j + 1, 1)]
                top = ref[part, plane, row(4, CY)]
                bottom = ref[part, plane, row(4, 1)]
                extra = ref[part, plane, row(5, 1)]
                lane = lanes_of(top)
                old = ref[part, plane, row(4, 0)]
                ref[part, plane, row(4, 0)] = jnp.where(
                    (lane >= WIDE) & (lane < 3 * WIDE), pltpu.roll(top, WIDE, 1), old)
                old = ref[part, plane, row(4, CY + 1)]
                ref[part, plane, row(4, CY + 1)] = jnp.where(
                    lane < 2 * WIDE, pltpu.roll(bottom, LANES - WIDE, 1),
                    jnp.where(lane < 3 * WIDE, pltpu.roll(extra, 2 * WIDE, 1), old))
                old = ref[part, plane, row(5, 0)]
                ref[part, plane, row(5, 0)] = jnp.where(lane < WIDE, pltpu.roll(top, LANES - 2 * WIDE, 1), old)

        for plane in range(1, PLANES - 1):
            across(plane)

    def mix(self, ref, plane, rows):
        for part in range(2):
            for at in rows:
                below, above = slice(at.start - 1, at.stop - 1), slice(at.start + 1, at.stop + 1)
                mixed = ref[part, plane, below] + ref[part, plane, above] + MIDDLE * ref[part, plane, at]
                self.u_ref[part, plane, at] = (
                    pltpu.roll(mixed, 1, 1) + pltpu.roll(mixed, LANES - 1, 1) + MIDDLE * mixed)

    def smoothed(self, part, plane, at):
        u_ref = self.u_ref
        return u_ref[part, plane - 1, at] + u_ref[part, plane + 1, at] + MIDDLE * u_ref[part, plane, at]

    def sweep(self, ref, first, last, body, rows):
        for plane in range(1, first + 2):
            self.mix(ref, plane, rows)
        for plane in range(first, last + 1):
            body(plane, rows)
            if plane + 2 < PLANES - 1:
                self.mix(ref, plane + 2, rows)

    def precondition(self, ref, right_ref):
        w_ref = self.w_ref
        for part in range(2):
            ref[part, :, 0:BASE] = jnp.zeros((PLANES, BASE, LANES), jnp.float32)
            ref[part, :, ROWS - 8:ROWS] = jnp.zeros((PLANES, 8, LANES), jnp.float32)

        def start(plane):
            for at in tiles():
                r_re, r_im = right_ref[0, plane, at], right_ref[1, plane, at]
                w_re, w_im = w_ref[0, plane, at], w_ref[1, plane, at]
                ref[0, plane, at] = w_re * r_re - w_im * r_im
                ref[1, plane, at] = w_re * r_im + w_im * r_re

        def update(plane, rows):
            for at in rows:
                z_re, z_im = ref[0, plane, at], ref[1, plane, at]
                w_re, w_im = w_ref[0, plane, at], w_ref[1, plane, at]
                g_re = (right_ref[0, plane, at] + self.smoothed(0, plane, at)) - PIVOT * z_re
                g_im = (right_ref[1, plane, at] + self.smoothed(1, plane, at)) - PIVOT * z_im
                ref[0, plane, at] = (1.0 - RELAX) * z_re + (w_re * g_re - w_im * g_im)
                ref[1, plane, at] = (1.0 - RELAX) * z_im + (w_re * g_im + w_im * g_re)

        for plane in range(1, PLANES - 1):
            start(plane)

        @pl.loop(0, SWEEPS - 2)
        def _(number):
            self.sweep(ref, 1, PLANES - 2, update, tiles())

        self.sweep(ref, 2, PLANES - 3, update, own_tiles())
        self.swap_ends(ref)
        self.swap_sides(ref)

    def image(self, ref, out_ref):
        d_ref = self.d_ref

        def body(plane, rows):
            for at in rows:
                z_re, z_im = ref[0, plane, at], ref[1, plane, at]
                d_re, d_im = d_ref[0, plane, at], d_ref[1, plane, at]
                out_ref[0, plane, at] = (d_re * z_re - d_im * z_im) - self.smoothed(0, plane, at)
                out_ref[1, plane, at] = (d_re * z_im + d_im * z_re) - self.smoothed(1, plane, at)

        self.sweep(ref, 2, PLANES - 3, body, own_tiles())


def tiles():
    return [slice(BASE + t * TILE, BASE + (t + 1) * TILE) for t in range(TILES)]


def own_tiles():
    return [slice(first_row(slot) + 1, first_row(slot) + 1 + CY) for slot in range(SLOTS)]


def send_back(ref, back_ref, first):
    for part in range(2):
        for slot in range(SLOTS):
            rows = slice(first_row(slot) + 1, first_row(slot) + 1 + CY)
            turned = ref[part, 2:2 + CX, rows].reshape(LANES, LANES).T
            for unit in range(GROUP):
                if slot_of(unit)[0] == slot:
                    at = slot_of(unit)[1] * WIDE + OWN
                    back_ref[unit, first + part * SLAB:first + (part + 1) * SLAB] = turned[at:at + SLAB]


def solve_kernel(got_ref, below_ref, above_ref, back_ref, sums_ref, r_ref, w_ref, d_ref, q_ref, z_ref, u_ref, turn_ref, turned_ref):
    is_first, is_last = position()
    low_at = jnp.where(is_first, 0, 3)
    high_at = jnp.where(is_last, 30, 27)

    turn_ref[...] = jnp.zeros_like(turn_ref)
    for ref in (r_ref, w_ref, d_ref, q_ref):
        for plane in range(1, PLANES - 1):
            for part in range(2):
                ref[part, plane, BODY] = jnp.zeros((TILES * TILE, LANES), jnp.float32)

    for unit in range(GROUP):
        slot, group = slot_of(unit)
        at = group * WIDE
        for field in range(FIELDS):
            turn_ref[slot, field, pl.ds(at + low_at, DEEP)] = below_ref[unit, field]
            turn_ref[slot, field, at + OWN:at + OWN + SLAB] = got_ref[unit, field]
            turn_ref[slot, field, pl.ds(at + high_at, DEEP)] = above_ref[unit, field]

    def fix(targets):
        for unit in range(GROUP):
            slot, group = slot_of(unit)
            at = group * WIDE
            for field in range(FIELDS):
                for target, ref, source in targets:
                    if ref is None:
                        row = jnp.zeros((1, LANES), jnp.float32)
                    else:
                        row = ref[unit, field, source:source + 1]
                    turn_ref[slot, field, at + target:at + target + 1] = row

    @pl.when(is_first)
    def _():
        fix(((8, got_ref, 0), (9, None, 0), (10, below_ref, DEEP - 1)))

    @pl.when(is_last)
    def _():
        fix(((27, above_ref, 0), (28, None, 0), (29, got_ref, SLAB - 1)))

    for slot in range(SLOTS):
        for field in range(FIELDS):
            turned_ref[slot, field] = turn_ref[slot, field].T

    def fill(plane, carry):
        at = pl.ds(pl.multiple_of(plane * TILE, TILE), TILE)
        for slot in range(SLOTS):
            b_re, b_im, kappa, damping = [turned_ref[slot, field, at] for field in range(FIELDS)]
            rows = slice(first_row(slot) + 1, first_row(slot) + 1 + CY)
            d_re = CENTER - kappa
            d_im = kappa * damping
            p_re = d_re - MIDDLE
            factor = jnp.where(kappa > 0, (RELAX / SCALE) / (p_re * p_re + d_im * d_im), 0.0)
            r_ref[0, 2 + plane, rows] = SCALE * b_re
            r_ref[1, 2 + plane, rows] = SCALE * b_im
            w_ref[0, 2 + plane, rows] = factor * p_re
            w_ref[1, 2 + plane, rows] = -factor * d_im
            d_ref[0, 2 + plane, rows] = SCALE * d_re
            d_ref[1, 2 + plane, rows] = SCALE * d_im
        return carry

    lax.fori_loop(0, CX, fill, 0, unroll=4)

    steps = Steps(u_ref, w_ref, d_ref)
    steps.swap_sides(r_ref)
    steps.swap_sides(w_ref)
    steps.precondition(z_ref, r_ref)
    send_back(z_ref, back_ref, 0)
    steps.image(z_ref, q_ref)
    steps.swap_ends(q_ref)
    steps.swap_sides(q_ref)
    steps.precondition(z_ref, q_ref)
    send_back(z_ref, back_ref, 2 * SLAB)
    steps.image(z_ref, w_ref)

    lane = lax.broadcasted_iota(jnp.int32, (TILE, LANES), 1)
    place = lax.rem(lane, WIDE)
    in_slab = (place >= OWN) & (place < OWN + SLAB)

    def over_cells(terms, count):
        sums = [jnp.zeros((TILE, LANES), jnp.float32)] * count
        for slot, at in enumerate(own_tiles()):
            here = terms(2, at)
            for plane in range(3, 2 + CX):
                here = [a + b for a, b in zip(here, terms(plane, at))]
            keep = in_slab if slot < SLOTS - 1 else in_slab & (lane < WIDE)
            sums = [a + jnp.where(keep, b, 0.0) for a, b in zip(sums, here)]
        return [total(v) for v in sums]

    def first_terms(plane, at):
        q_re, q_im = q_ref[0, plane, at], q_ref[1, plane, at]
        b_re, b_im = r_ref[0, plane, at], r_ref[1, plane, at]
        t_re, t_im = w_ref[0, plane, at], w_ref[1, plane, at]
        return (q_re * q_re + q_im * q_im, q_re * b_re + q_im * b_im, q_re * b_im - q_im * b_re,
                q_re * t_re + q_im * t_im, q_re * t_im - q_im * t_re)

    norm, proj_re, proj_im, cross_re, cross_im = over_cells(first_terms, 5)
    safe = jnp.where(norm > 0, norm, 1.0)
    cross_re = cross_re / safe
    cross_im = cross_im / safe
    mean_re = jnp.broadcast_to(cross_re, (TILE, LANES))
    mean_im = jnp.broadcast_to(cross_im, (TILE, LANES))

    def second_terms(plane, at):
        q_re, q_im = q_ref[0, plane, at], q_ref[1, plane, at]
        b_re, b_im = r_ref[0, plane, at], r_ref[1, plane, at]
        p_re = w_ref[0, plane, at] - (mean_re * q_re - mean_im * q_im)
        p_im = w_ref[1, plane, at] - (mean_re * q_im + mean_im * q_re)
        return p_re * p_re + p_im * p_im, p_re * b_re + p_im * b_im, p_re * b_im - p_im * b_re

    rest, pair_re, pair_im = over_cells(second_terms, 3)
    row = lax.broadcasted_iota(jnp.int32, (STATS, LANES), 0)
    table = jnp.zeros((STATS, LANES), jnp.float32)
    for n, value in enumerate((norm, proj_re, proj_im, cross_re, cross_im, rest, pair_re, pair_im)):
        table = jnp.where(row == n, value, table)

    for target in range(PZ):
        sums_ref[target] = table


def merged(rows):
    norm, proj_re, proj_im, cross_re, cross_im, rest, pair_re, pair_im = rows

    def over(values):
        return jnp.sum(values, axis=0, keepdims=True)

    whole = over(norm)
    mean_re = over(norm * cross_re) / whole
    mean_im = over(norm * cross_im) / whole
    off_re = cross_re - mean_re
    off_im = cross_im - mean_im
    return (whole, over(proj_re), over(proj_im), mean_re, mean_im,
            over(rest + norm * (off_re * off_re + off_im * off_im)),
            over(pair_re + off_re * proj_re + off_im * proj_im),
            over(pair_im + off_re * proj_im - off_im * proj_re))


def pack_kernel(table_ref, back_ref, out_ref):
    for n, value in enumerate(merged([table_ref[:, n] for n in range(STATS)])):
        for unit in range(GROUP):
            out_ref[unit, FIELDS * SLAB + n:FIELDS * SLAB + n + 1] = value
    for unit in range(GROUP):
        out_ref[unit, 0:FIELDS * SLAB] = back_ref[unit]


def finish_kernel(back_ref, wave_ref, damping_ref, solution_ref, shares_ref):
    rows = [back_ref[:, FIELDS * SLAB + n] for n in range(STATS)]
    norm, proj_re, proj_im, mean_re, mean_im, size, pair_re, pair_im = merged(rows)
    beta_re = pair_re / size
    beta_im = pair_im / size
    lead_re = proj_re / norm - (beta_re * mean_re - beta_im * mean_im)
    lead_im = proj_im / norm - (beta_re * mean_im + beta_im * mean_re)
    shape = (SLAB, LANES)
    beta_re, beta_im, lead_re, lead_im = [jnp.broadcast_to(v, shape) for v in (beta_re, beta_im, lead_re, lead_im)]
    per = LANES // SLAB
    odd, turn = path()
    for tile in range(CZ // LANES):
        pieces = [[], []]
        for source in range(tile * per, (tile + 1) * per):
            at = device_of(source, odd, turn)
            f_re, f_im, s_re, s_im = [back_ref[at, n * SLAB:(n + 1) * SLAB] for n in range(FIELDS)]
            pieces[0].append((lead_re * f_re - lead_im * f_im) + (beta_re * s_re - beta_im * s_im))
            pieces[1].append((lead_re * f_im + lead_im * f_re) + (beta_re * s_im + beta_im * s_re))
        here = slice(tile * LANES, (tile + 1) * LANES)
        x_re, x_im = [jnp.concatenate(p, axis=0).T.reshape(CX, CY, LANES) for p in pieces]
        solution_ref[0, :, :, here] = x_re
        solution_ref[1, :, :, here] = x_im
        u_re, u_im = wave_ref[0, :, :, here], wave_ref[1, :, :, here]
        shares_ref[:, :, here] = (u_re * x_re + u_im * x_im) - damping_ref[:, :, here] * (u_im * x_re - u_re * x_im)


def moved(values, step):
    shots = lax.axis_size("shot")
    pairs = []
    for turn in range(shots):
        chain = []
        for layer in range(PZ):
            odd = layer % 2
            for slab in range(GROUP):
                if slab < RING:
                    device = odd * RING + (turn + 1 + slab) % RING
                else:
                    device = (1 - odd) * RING + (turn - slab) % RING
                chain.append((layer * GROUP + device) * shots + turn)
        pairs += list(zip(chain, chain[1:]) if step > 0 else zip(chain[1:], chain))
    return lax.ppermute(values, ("sub", "shot"), pairs)


def call(kernel, out_shapes, scratch=(), space=pltpu.VMEM, limit=VMEM_LIMIT):
    one = pl.BlockSpec(memory_space=pltpu.VMEM)
    given = pl.BlockSpec(memory_space=space)

    def run(*args):
        return pl.pallas_call(
            kernel,
            out_shape=[jax.ShapeDtypeStruct(shape, jnp.float32) for shape in out_shapes],
            in_specs=[given] * len(args),
            out_specs=[one] * len(out_shapes),
            scratch_shapes=list(scratch),
            compiler_params=pltpu.CompilerParams(vmem_limit_bytes=limit),
        )(*args)

    return run


def local(adjoint_source, forward_field, kappa, damping):
    source = adjoint_source[0, :, 0]
    wave = forward_field[0, :, 0]
    kappa = kappa[0]
    damping = damping[0]
    block = (CX, CY, CZ)
    held = [pltpu.VMEM(shape, jnp.float32) for shape in ((2,) + block, block, block, (FIELDS, CZ, LANES))]
    message, = call(turn_kernel, [(GROUP, FIELDS, SLAB, LANES)], held + [pltpu.SemaphoreType.DMA((FIELDS,))],
                    pltpu.HBM, 60 * 1024 * 1024)(source, kappa, damping)
    layers = [[k * GROUP + n for n in range(GROUP)] for k in range(PZ)]
    columns = [[k * GROUP + n for k in range(PZ)] for n in range(GROUP)]
    got = lax.all_to_all(message, "sub", 0, 0, axis_index_groups=layers)
    edge = (GROUP, FIELDS, DEEP, LANES)
    low, high = call(edges_kernel, [edge, edge])(got)
    below = moved(high, 1)
    above = moved(low, -1)
    work = pltpu.VMEM((2, PLANES, ROWS, LANES), jnp.float32)
    turn = pltpu.VMEM((SLOTS, FIELDS, LANES, LANES), jnp.float32)
    back, sums = call(solve_kernel, [(GROUP, FIELDS * SLAB, LANES), (PZ, STATS, LANES)],
                      [work] * 6 + [turn] * 2)(got, below, above)
    table = lax.all_to_all(sums, "sub", 0, 0, axis_index_groups=columns)
    back, = call(pack_kernel, [(GROUP, BACK, LANES)])(table, back)
    back = lax.all_to_all(back, "sub", 0, 0, axis_index_groups=layers)
    solved, shares = call(finish_kernel, [(2, CX, CY, CZ), (CX, CY, CZ)])(back, wave, damping)
    shots = lax.axis_size("shot")
    shares = shares.reshape(shots, CX // shots, CY, CZ)
    share = jnp.sum(lax.all_to_all(shares, "shot", 0, 0), axis=0)
    return (solved[None, :, None], share[None])


def solution(mesh):
    return jax.shard_map(
        local,
        mesh=mesh,
        in_specs=(
            P("shot", None, "sub", None, None, None),
            P("shot", None, "sub", None, None, None),
            P("sub", None, None, None),
            P("sub", None, None, None),
        ),
        out_specs=(P("shot", None, "sub", None, None, None), P("sub", "shot", None, None)),
        check_vma=False,
    )
```

```python
import jax
import jax.numpy as jnp
from jax import lax
from jax.experimental import pallas as pl
from jax.experimental.pallas import tpu as pltpu
from jax.sharding import PartitionSpec as P

SWEEPS = 4
PX = 4
PY = 4
PZ = 4
CX = 16
CY = 8
CZ = 256
CENTER = 13.5
RELAX = 0.7

SCALE = 16.0
MIDDLE = 4.0
PIVOT = 64.0

GROUP = PX * PY
SLAB = CZ // GROUP
RING = GROUP // 2
DEEP = 8
LANES = 128
TILE = 8

PLANES = CX + 4
SLOT = CY + 3
SLOTS = 6
TILES = 8
BASE = 8
ROWS = BASE + TILES * TILE + 8
BODY = slice(BASE, BASE + TILES * TILE)
WIDE = 40
OWN = 11
FIELDS = 4
STATS = 8
BACK = FIELDS * SLAB + STATS
VMEM_LIMIT = 24 * 1024 * 1024


def slot_of(unit):
    i, j = unit % PX, unit // PX
    if i < PX - 1:
        return j, i
    return (PX, j) if j < PY - 1 else (PX + 1, 0)


def first_row(slot):
    return BASE + SLOT * slot


def lanes_of(values):
    return lax.broadcasted_iota(jnp.int32, values.shape, values.ndim - 1)


def turn_kernel(source_ref, kappa_ref, damping_ref, out_ref, source_held, kappa_held, damping_held, turned_ref, sems):
    copies = [pltpu.make_async_copy(source_ref.at[0], source_held.at[0], sems.at[0]),
              pltpu.make_async_copy(source_ref.at[1], source_held.at[1], sems.at[1]),
              pltpu.make_async_copy(kappa_ref, kappa_held, sems.at[2]),
              pltpu.make_async_copy(damping_ref, damping_held, sems.at[3])]
    for copy in copies:
        copy.start()
    odd, turn = path()
    for field in range(FIELDS):
        copies[field].wait()
        held = (source_held.at[0], source_held.at[1], kappa_held, damping_held)[field]
        for tile in range(CZ // LANES):
            here = slice(tile * LANES, (tile + 1) * LANES)
            turned_ref[field, here] = held[:, :, here].reshape(LANES, LANES).T
    for device in range(GROUP):
        rows = pl.ds(pl.multiple_of(slab_of(device, odd, turn) * SLAB, SLAB), SLAB)
        for field in range(FIELDS):
            out_ref[device, field] = turned_ref[field, rows]


def edges_kernel(got_ref, low_ref, high_ref):
    low_ref[...] = got_ref[:, :, 0:DEEP]
    high_ref[...] = got_ref[:, :, SLAB - DEEP:SLAB]


def total(values):
    return jnp.sum(jnp.sum(values, axis=0, keepdims=True), axis=1, keepdims=True)


def path():
    return lax.rem(lax.axis_index("sub") // GROUP, 2), lax.axis_index("shot")


def slab_of(device, odd, turn):
    half, y = (divmod(device, RING) if isinstance(device, int) else (device // RING, lax.rem(device, RING)))
    there = lax.rem(y - turn - 1 + 2 * RING, RING)
    back = RING + lax.rem(turn - y + 2 * RING, RING)
    return jnp.where(half == odd, there, back)


def device_of(slab, odd, turn):
    if slab < RING:
        return odd * RING + lax.rem(turn + 1 + slab, RING)
    return (1 - odd) * RING + lax.rem(turn - slab + 3 * RING, RING)


def position():
    odd, turn = path()
    place = slab_of(lax.rem(lax.axis_index("sub"), GROUP), odd, turn)
    return place == 0, place == GROUP - 1


class Steps:

    def __init__(self, u_ref, w_ref, d_ref):
        self.is_first, self.is_last = position()
        self.u_ref, self.w_ref, self.d_ref = u_ref, w_ref, d_ref
        for part in range(2):
            for plane in (0, PLANES - 1):
                u_ref[part, plane] = jnp.zeros((ROWS, LANES), jnp.float32)

    def swap_ends(self, ref):
        def run(a, b):
            lane = lax.broadcasted_iota(jnp.int32, (TILE, LANES), 1)
            place = lax.rem(lane, WIDE)
            source = jnp.where(place == a, lane + 3, jnp.where(place == b, lane - 3, lane))
            source = jnp.minimum(source, LANES - 1)
            for plane in range(2, 2 + CX):
                for part in range(2):
                    for at in own_tiles():
                        ref[part, plane, at] = jnp.take_along_axis(ref[part, plane, at], source, axis=1)

        @pl.when(self.is_first)
        def _():
            run(8, 10)

        @pl.when(self.is_last)
        def _():
            run(27, 29)

    def swap_sides(self, ref):
        one = jnp.zeros((TILE, LANES), jnp.float32)
        lane = lanes_of(one)
        last, first = CX + 1, 2

        def rows(slot):
            return slice(first_row(slot) + 1, first_row(slot) + 1 + CY)

        for part in range(2):
            for j in range(PY):
                here = rows(j)
                moved_up = pltpu.roll(ref[part, last, here], WIDE, 1)
                ref[part, 1, here] = jnp.where((lane >= WIDE) & (lane < 3 * WIDE), moved_up, ref[part, 1, here])
                slot, group = slot_of(PX - 1 + PX * j)
                end = rows(slot)
                inside = (lane >= group * WIDE) & (lane < (group + 1) * WIDE)
                shift = (2 - group) * WIDE
                moved_down = pltpu.roll(ref[part, first, here], LANES - WIDE, 1)
                from_end = pltpu.roll(ref[part, first, end], shift, 1) if shift else ref[part, first, end]
                ref[part, PLANES - 2, here] = jnp.where(
                    lane < 2 * WIDE, moved_down, jnp.where(lane < 3 * WIDE, from_end, ref[part, PLANES - 2, here]))
                to_end = ref[part, last, here]
                to_end = pltpu.roll(to_end, LANES - shift, 1) if shift else to_end
                ref[part, 1, end] = jnp.where(inside, to_end, ref[part, 1, end])

        def across(plane):
            for part in range(2):
                def row(slot, n):
                    return slice(first_row(slot) + n, first_row(slot) + n + 1)

                for j in range(PY):
                    if j > 0:
                        ref[part, plane, row(j, 0)] = ref[part, plane, row(j - 1, CY)]
                    if j < PY - 1:
                        ref[part, plane, row(j, CY + 1)] = ref[part, plane, row(j + 1, 1)]
                top = ref[part, plane, row(4, CY)]
                bottom = ref[part, plane, row(4, 1)]
                extra = ref[part, plane, row(5, 1)]
                lane = lanes_of(top)
                old = ref[part, plane, row(4, 0)]
                ref[part, plane, row(4, 0)] = jnp.where(
                    (lane >= WIDE) & (lane < 3 * WIDE), pltpu.roll(top, WIDE, 1), old)
                old = ref[part, plane, row(4, CY + 1)]
                ref[part, plane, row(4, CY + 1)] = jnp.where(
                    lane < 2 * WIDE, pltpu.roll(bottom, LANES - WIDE, 1),
                    jnp.where(lane < 3 * WIDE, pltpu.roll(extra, 2 * WIDE, 1), old))
                old = ref[part, plane, row(5, 0)]
                ref[part, plane, row(5, 0)] = jnp.where(lane < WIDE, pltpu.roll(top, LANES - 2 * WIDE, 1), old)

        for plane in range(1, PLANES - 1):
            across(plane)

    def mix(self, ref, plane, rows):
        for part in range(2):
            for at in rows:
                below, above = slice(at.start - 1, at.stop - 1), slice(at.start + 1, at.stop + 1)
                mixed = ref[part, plane, below] + ref[part, plane, above] + MIDDLE * ref[part, plane, at]
                self.u_ref[part, plane, at] = (
                    pltpu.roll(mixed, 1, 1) + pltpu.roll(mixed, LANES - 1, 1) + MIDDLE * mixed)

    def smoothed(self, part, plane, at):
        u_ref = self.u_ref
        return u_ref[part, plane - 1, at] + u_ref[part, plane + 1, at] + MIDDLE * u_ref[part, plane, at]

    def sweep(self, ref, first, last, body, rows):
        for plane in range(1, first + 2):
            self.mix(ref, plane, rows)
        for plane in range(first, last + 1):
            body(plane, rows)
            if plane + 2 < PLANES - 1:
                self.mix(ref, plane + 2, rows)

    def precondition(self, ref, right_ref):
        w_ref = self.w_ref
        for part in range(2):
            ref[part, :, 0:BASE] = jnp.zeros((PLANES, BASE, LANES), jnp.float32)
            ref[part, :, ROWS - 8:ROWS] = jnp.zeros((PLANES, 8, LANES), jnp.float32)

        def start(plane):
            for at in tiles():
                r_re, r_im = right_ref[0, plane, at], right_ref[1, plane, at]
                w_re, w_im = w_ref[0, plane, at], w_ref[1, plane, at]
                ref[0, plane, at] = w_re * r_re - w_im * r_im
                ref[1, plane, at] = w_re * r_im + w_im * r_re

        def update(plane, rows):
            for at in rows:
                z_re, z_im = ref[0, plane, at], ref[1, plane, at]
                w_re, w_im = w_ref[0, plane, at], w_ref[1, plane, at]
                g_re = (right_ref[0, plane, at] + self.smoothed(0, plane, at)) - PIVOT * z_re
                g_im = (right_ref[1, plane, at] + self.smoothed(1, plane, at)) - PIVOT * z_im
                ref[0, plane, at] = (1.0 - RELAX) * z_re + (w_re * g_re - w_im * g_im)
                ref[1, plane, at] = (1.0 - RELAX) * z_im + (w_re * g_im + w_im * g_re)

        for plane in range(1, PLANES - 1):
            start(plane)

        @pl.loop(0, SWEEPS - 2)
        def _(number):
            self.sweep(ref, 1, PLANES - 2, update, tiles())

        self.sweep(ref, 2, PLANES - 3, update, own_tiles())
        self.swap_ends(ref)
        self.swap_sides(ref)

    def image(self, ref, out_ref):
        d_ref = self.d_ref

        def body(plane, rows):
            for at in rows:
                z_re, z_im = ref[0, plane, at], ref[1, plane, at]
                d_re, d_im = d_ref[0, plane, at], d_ref[1, plane, at]
                out_ref[0, plane, at] = (d_re * z_re - d_im * z_im) - self.smoothed(0, plane, at)
                out_ref[1, plane, at] = (d_re * z_im + d_im * z_re) - self.smoothed(1, plane, at)

        self.sweep(ref, 2, PLANES - 3, body, own_tiles())


def tiles():
    return [slice(BASE + t * TILE, BASE + (t + 1) * TILE) for t in range(TILES)]


def own_tiles():
    return [slice(first_row(slot) + 1, first_row(slot) + 1 + CY) for slot in range(SLOTS)]


def send_back(ref, back_ref, first):
    for part in range(2):
        for slot in range(SLOTS):
            rows = slice(first_row(slot) + 1, first_row(slot) + 1 + CY)
            turned = ref[part, 2:2 + CX, rows].reshape(LANES, LANES).T
            for unit in range(GROUP):
                if slot_of(unit)[0] == slot:
                    at = slot_of(unit)[1] * WIDE + OWN
                    back_ref[unit, first + part * SLAB:first + (part + 1) * SLAB] = turned[at:at + SLAB]


def solve_kernel(got_ref, below_ref, above_ref, back_ref, sums_ref, r_ref, w_ref, d_ref, q_ref, z_ref, u_ref, turn_ref, turned_ref):
    is_first, is_last = position()
    low_at = jnp.where(is_first, 0, 3)
    high_at = jnp.where(is_last, 30, 27)

    turn_ref[...] = jnp.zeros_like(turn_ref)
    for ref in (r_ref, w_ref, q_ref):
        for plane in range(1, PLANES - 1):
            for part in range(2):
                ref[part, plane, BODY] = jnp.zeros((TILES * TILE, LANES), jnp.float32)

    for unit in range(GROUP):
        slot, group = slot_of(unit)
        at = group * WIDE
        for field in range(FIELDS):
            turn_ref[slot, field, pl.ds(at + low_at, DEEP)] = below_ref[unit, field]
            turn_ref[slot, field, at + OWN:at + OWN + SLAB] = got_ref[unit, field]
            turn_ref[slot, field, pl.ds(at + high_at, DEEP)] = above_ref[unit, field]

    def fix(targets):
        for unit in range(GROUP):
            slot, group = slot_of(unit)
            at = group * WIDE
            for field in range(FIELDS):
                for target, ref, source in targets:
                    if ref is None:
                        row = jnp.zeros((1, LANES), jnp.float32)
                    else:
                        row = ref[unit, field, source:source + 1]
                    turn_ref[slot, field, at + target:at + target + 1] = row

    @pl.when(is_first)
    def _():
        fix(((8, got_ref, 0), (9, None, 0), (10, below_ref, DEEP - 1)))

    @pl.when(is_last)
    def _():
        fix(((27, above_ref, 0), (28, None, 0), (29, got_ref, SLAB - 1)))

    for slot in range(SLOTS):
        for field in range(FIELDS):
            turned_ref[slot, field] = turn_ref[slot, field].T

    def fill(plane, carry):
        at = pl.ds(pl.multiple_of(plane * TILE, TILE), TILE)
        for slot in range(SLOTS):
            b_re, b_im, kappa, damping = [turned_ref[slot, field, at] for field in range(FIELDS)]
            rows = slice(first_row(slot) + 1, first_row(slot) + 1 + CY)
            d_re = CENTER - kappa
            d_im = kappa * damping
            p_re = d_re - MIDDLE
            factor = jnp.where(kappa > 0, (RELAX / SCALE) / (p_re * p_re + d_im * d_im), 0.0)
            r_ref[0, 2 + plane, rows] = SCALE * b_re
            r_ref[1, 2 + plane, rows] = SCALE * b_im
            w_ref[0, 2 + plane, rows] = factor * p_re
            w_ref[1, 2 + plane, rows] = -factor * d_im
            d_ref[0, 2 + plane, rows] = SCALE * d_re
            d_ref[1, 2 + plane, rows] = SCALE * d_im
        return carry

    lax.fori_loop(0, CX, fill, 0, unroll=4)

    steps = Steps(u_ref, w_ref, d_ref)
    steps.swap_sides(r_ref)
    steps.swap_sides(w_ref)
    steps.precondition(z_ref, r_ref)
    send_back(z_ref, back_ref, 0)
    steps.image(z_ref, q_ref)
    steps.swap_ends(q_ref)
    steps.swap_sides(q_ref)
    steps.precondition(z_ref, q_ref)
    send_back(z_ref, back_ref, 2 * SLAB)
    steps.image(z_ref, w_ref)

    lane = lax.broadcasted_iota(jnp.int32, (TILE, LANES), 1)
    place = lax.rem(lane, WIDE)
    in_slab = (place >= OWN) & (place < OWN + SLAB)

    def over_cells(terms, count):
        sums = [jnp.zeros((TILE, LANES), jnp.float32)] * count
        for slot, at in enumerate(own_tiles()):
            here = terms(2, at)
            for plane in range(3, 2 + CX):
                here = [a + b for a, b in zip(here, terms(plane, at))]
            keep = in_slab if slot < SLOTS - 1 else in_slab & (lane < WIDE)
            sums = [a + jnp.where(keep, b, 0.0) for a, b in zip(sums, here)]
        return [total(v) for v in sums]

    def first_terms(plane, at):
        q_re, q_im = q_ref[0, plane, at], q_ref[1, plane, at]
        b_re, b_im = r_ref[0, plane, at], r_ref[1, plane, at]
        t_re, t_im = w_ref[0, plane, at], w_ref[1, plane, at]
        return (q_re * q_re + q_im * q_im, q_re * b_re + q_im * b_im, q_re * b_im - q_im * b_re,
                q_re * t_re + q_im * t_im, q_re * t_im - q_im * t_re)

    norm, proj_re, proj_im, cross_re, cross_im = over_cells(first_terms, 5)
    safe = jnp.where(norm > 0, norm, 1.0)
    cross_re = cross_re / safe
    cross_im = cross_im / safe
    mean_re = jnp.broadcast_to(cross_re, (TILE, LANES))
    mean_im = jnp.broadcast_to(cross_im, (TILE, LANES))

    def second_terms(plane, at):
        q_re, q_im = q_ref[0, plane, at], q_ref[1, plane, at]
        b_re, b_im = r_ref[0, plane, at], r_ref[1, plane, at]
        p_re = w_ref[0, plane, at] - (mean_re * q_re - mean_im * q_im)
        p_im = w_ref[1, plane, at] - (mean_re * q_im + mean_im * q_re)
        return p_re * p_re + p_im * p_im, p_re * b_re + p_im * b_im, p_re * b_im - p_im * b_re

    rest, pair_re, pair_im = over_cells(second_terms, 3)
    row = lax.broadcasted_iota(jnp.int32, (STATS, LANES), 0)
    table = jnp.zeros((STATS, LANES), jnp.float32)
    for n, value in enumerate((norm, proj_re, proj_im, cross_re, cross_im, rest, pair_re, pair_im)):
        table = jnp.where(row == n, value, table)

    for target in range(PZ):
        sums_ref[target] = table


def merged(rows):
    norm, proj_re, proj_im, cross_re, cross_im, rest, pair_re, pair_im = rows

    def over(values):
        return jnp.sum(values, axis=0, keepdims=True)

    whole = over(norm)
    mean_re = over(norm * cross_re) / whole
    mean_im = over(norm * cross_im) / whole
    off_re = cross_re - mean_re
    off_im = cross_im - mean_im
    return (whole, over(proj_re), over(proj_im), mean_re, mean_im,
            over(rest + norm * (off_re * off_re + off_im * off_im)),
            over(pair_re + off_re * proj_re + off_im * proj_im),
            over(pair_im + off_re * proj_im - off_im * proj_re))


def pack_kernel(table_ref, back_ref, out_ref):
    for n, value in enumerate(merged([table_ref[:, n] for n in range(STATS)])):
        for unit in range(GROUP):
            out_ref[unit, FIELDS * SLAB + n:FIELDS * SLAB + n + 1] = value
    for unit in range(GROUP):
        out_ref[unit, 0:FIELDS * SLAB] = back_ref[unit]


def finish_kernel(back_ref, wave_ref, damping_ref, solution_ref, shares_ref):
    rows = [back_ref[:, FIELDS * SLAB + n] for n in range(STATS)]
    norm, proj_re, proj_im, mean_re, mean_im, size, pair_re, pair_im = merged(rows)
    beta_re = pair_re / size
    beta_im = pair_im / size
    lead_re = proj_re / norm - (beta_re * mean_re - beta_im * mean_im)
    lead_im = proj_im / norm - (beta_re * mean_im + beta_im * mean_re)
    shape = (SLAB, LANES)
    beta_re, beta_im, lead_re, lead_im = [jnp.broadcast_to(v, shape) for v in (beta_re, beta_im, lead_re, lead_im)]
    per = LANES // SLAB
    odd, turn = path()
    for tile in range(CZ // LANES):
        pieces = [[], []]
        for source in range(tile * per, (tile + 1) * per):
            at = device_of(source, odd, turn)
            f_re, f_im, s_re, s_im = [back_ref[at, n * SLAB:(n + 1) * SLAB] for n in range(FIELDS)]
            pieces[0].append((lead_re * f_re - lead_im * f_im) + (beta_re * s_re - beta_im * s_im))
            pieces[1].append((lead_re * f_im + lead_im * f_re) + (beta_re * s_im + beta_im * s_re))
        here = slice(tile * LANES, (tile + 1) * LANES)
        x_re, x_im = [jnp.concatenate(p, axis=0).T.reshape(CX, CY, LANES) for p in pieces]
        solution_ref[0, :, :, here] = x_re
        solution_ref[1, :, :, here] = x_im
        u_re, u_im = wave_ref[0, :, :, here], wave_ref[1, :, :, here]
        shares_ref[:, :, here] = (u_re * x_re + u_im * x_im) - damping_ref[:, :, here] * (u_im * x_re - u_re * x_im)


def moved(values, step):
    shots = lax.axis_size("shot")
    pairs = []
    for turn in range(shots):
        chain = []
        for layer in range(PZ):
            odd = layer % 2
            for slab in range(GROUP):
                if slab < RING:
                    device = odd * RING + (turn + 1 + slab) % RING
                else:
                    device = (1 - odd) * RING + (turn - slab) % RING
                chain.append((layer * GROUP + device) * shots + turn)
        pairs += list(zip(chain, chain[1:]) if step > 0 else zip(chain[1:], chain))
    return lax.ppermute(values, ("sub", "shot"), pairs)


def call(kernel, out_shapes, scratch=(), space=pltpu.VMEM, limit=VMEM_LIMIT):
    one = pl.BlockSpec(memory_space=pltpu.VMEM)
    given = pl.BlockSpec(memory_space=space)

    def run(*args):
        return pl.pallas_call(
            kernel,
            out_shape=[jax.ShapeDtypeStruct(shape, jnp.float32) for shape in out_shapes],
            in_specs=[given] * len(args),
            out_specs=[one] * len(out_shapes),
            scratch_shapes=list(scratch),
            compiler_params=pltpu.CompilerParams(vmem_limit_bytes=limit),
        )(*args)

    return run


def local(adjoint_source, forward_field, kappa, damping):
    source = adjoint_source[0, :, 0]
    wave = forward_field[0, :, 0]
    kappa = kappa[0]
    damping = damping[0]
    block = (CX, CY, CZ)
    held = [pltpu.VMEM(shape, jnp.float32) for shape in ((2,) + block, block, block, (FIELDS, CZ, LANES))]
    message, = call(turn_kernel, [(GROUP, FIELDS, SLAB, LANES)], held + [pltpu.SemaphoreType.DMA((FIELDS,))],
                    pltpu.HBM, 60 * 1024 * 1024)(source, kappa, damping)
    layers = [[k * GROUP + n for n in range(GROUP)] for k in range(PZ)]
    columns = [[k * GROUP + n for k in range(PZ)] for n in range(GROUP)]
    got = lax.all_to_all(message, "sub", 0, 0, axis_index_groups=layers)
    edge = (GROUP, FIELDS, DEEP, LANES)
    low, high = call(edges_kernel, [edge, edge])(got)
    below = moved(high, 1)
    above = moved(low, -1)
    work = pltpu.VMEM((2, PLANES, ROWS, LANES), jnp.float32)
    turn = pltpu.VMEM((SLOTS, FIELDS, LANES, LANES), jnp.float32)
    back, sums = call(solve_kernel, [(GROUP, FIELDS * SLAB, LANES), (PZ, STATS, LANES)],
                      [work] * 6 + [turn] * 2)(got, below, above)
    table = lax.all_to_all(sums, "sub", 0, 0, axis_index_groups=columns)
    back, = call(pack_kernel, [(GROUP, BACK, LANES)])(table, back)
    back = lax.all_to_all(back, "sub", 0, 0, axis_index_groups=layers)
    solved, shares = call(finish_kernel, [(2, CX, CY, CZ), (CX, CY, CZ)])(back, wave, damping)
    shots = lax.axis_size("shot")
    shares = shares.reshape(shots, CX // shots, CY, CZ)
    share = jnp.sum(lax.all_to_all(shares, "shot", 0, 0), axis=0)
    return (solved[None, :, None], share[None])


def solution(mesh):
    return jax.shard_map(
        local,
        mesh=mesh,
        in_specs=(
            P("shot", None, "sub", None, None, None),
            P("shot", None, "sub", None, None, None),
            P("sub", None, None, None),
            P("sub", None, None, None),
        ),
        out_specs=(P("shot", None, "sub", None, None, None), P("sub", "shot", None, None)),
        check_vma=False,
    )
```

```python
import jax
import jax.numpy as jnp
from jax import lax
from jax.experimental import pallas as pl
from jax.experimental.pallas import tpu as pltpu
from jax.sharding import PartitionSpec as P

SWEEPS = 4
PX = 4
PY = 4
PZ = 4
CX = 16
CY = 8
CZ = 256
CENTER = 13.5
RELAX = 0.7

SCALE = 16.0
MIDDLE = 4.0
PIVOT = 64.0

GROUP = PX * PY
SLAB = CZ // GROUP
RING = GROUP // 2
DEEP = 8
LANES = 128
TILE = 8

PLANES = CX + 4
SLOT = CY + 3
SLOTS = 6
TILES = 8
BASE = 8
ROWS = BASE + TILES * TILE + 8
BODY = slice(BASE, BASE + TILES * TILE)
WIDE = 40
OWN = 11
FIELDS = 4
STATS = 8
BACK = FIELDS * SLAB + STATS
VMEM_LIMIT = 24 * 1024 * 1024


def slot_of(unit):
    i, j = unit % PX, unit // PX
    if i < PX - 1:
        return j, i
    return (PX, j) if j < PY - 1 else (PX + 1, 0)


def first_row(slot):
    return BASE + SLOT * slot


def lanes_of(values):
    return lax.broadcasted_iota(jnp.int32, values.shape, values.ndim - 1)


def turn_kernel(source_ref, kappa_ref, damping_ref, out_ref, source_held, kappa_held, damping_held, turned_ref, ready_ref, sems, out_sems):
    copies = [pltpu.make_async_copy(source_ref.at[0], source_held.at[0], sems.at[0]),
              pltpu.make_async_copy(source_ref.at[1], source_held.at[1], sems.at[1]),
              pltpu.make_async_copy(kappa_ref, kappa_held, sems.at[2]),
              pltpu.make_async_copy(damping_ref, damping_held, sems.at[3])]
    for copy in copies:
        copy.start()
    odd, turn = path()
    sent = []
    for field in range(FIELDS):
        copies[field].wait()
        held = (source_held.at[0], source_held.at[1], kappa_held, damping_held)[field]
        for tile in range(CZ // LANES):
            here = slice(tile * LANES, (tile + 1) * LANES)
            turned_ref[field, here] = held[:, :, here].reshape(LANES, LANES).T
        for device in range(GROUP):
            rows = pl.ds(pl.multiple_of(slab_of(device, odd, turn) * SLAB, SLAB), SLAB)
            ready_ref[field, device] = turned_ref[field, rows]
        sent.append(pltpu.make_async_copy(ready_ref.at[field], out_ref.at[:, field], out_sems.at[field]))
        sent[field].start()
    for copy in sent:
        copy.wait()


def edges_kernel(got_ref, low_ref, high_ref):
    low_ref[...] = got_ref[:, :, 0:DEEP]
    high_ref[...] = got_ref[:, :, SLAB - DEEP:SLAB]


def total(values):
    return jnp.sum(jnp.sum(values, axis=0, keepdims=True), axis=1, keepdims=True)


def path():
    return lax.rem(lax.axis_index("sub") // GROUP, 2), lax.axis_index("shot")


def slab_of(device, odd, turn):
    half, y = (divmod(device, RING) if isinstance(device, int) else (device // RING, lax.rem(device, RING)))
    there = lax.rem(y - turn - 1 + 2 * RING, RING)
    back = RING + lax.rem(turn - y + 2 * RING, RING)
    return jnp.where(half == odd, there, back)


def device_of(slab, odd, turn):
    if slab < RING:
        return odd * RING + lax.rem(turn + 1 + slab, RING)
    return (1 - odd) * RING + lax.rem(turn - slab + 3 * RING, RING)


def position():
    odd, turn = path()
    place = slab_of(lax.rem(lax.axis_index("sub"), GROUP), odd, turn)
    return place == 0, place == GROUP - 1


class Steps:

    def __init__(self, u_ref, w_ref, d_ref):
        self.is_first, self.is_last = position()
        self.u_ref, self.w_ref, self.d_ref = u_ref, w_ref, d_ref
        for part in range(2):
            for plane in (0, PLANES - 1):
                u_ref[part, plane] = jnp.zeros((ROWS, LANES), jnp.float32)

    def swap_ends(self, ref):
        def run(a, b):
            lane = lax.broadcasted_iota(jnp.int32, (TILE, LANES), 1)
            place = lax.rem(lane, WIDE)
            source = jnp.where(place == a, lane + 3, jnp.where(place == b, lane - 3, lane))
            source = jnp.minimum(source, LANES - 1)
            for plane in range(2, 2 + CX):
                for part in range(2):
                    for at in own_tiles():
                        ref[part, plane, at] = jnp.take_along_axis(ref[part, plane, at], source, axis=1)

        @pl.when(self.is_first)
        def _():
            run(8, 10)

        @pl.when(self.is_last)
        def _():
            run(27, 29)

    def swap_sides(self, ref):
        one = jnp.zeros((TILE, LANES), jnp.float32)
        lane = lanes_of(one)
        last, first = CX + 1, 2

        def rows(slot):
            return slice(first_row(slot) + 1, first_row(slot) + 1 + CY)

        for part in range(2):
            for j in range(PY):
                here = rows(j)
                moved_up = pltpu.roll(ref[part, last, here], WIDE, 1)
                ref[part, 1, here] = jnp.where((lane >= WIDE) & (lane < 3 * WIDE), moved_up, ref[part, 1, here])
                slot, group = slot_of(PX - 1 + PX * j)
                end = rows(slot)
                inside = (lane >= group * WIDE) & (lane < (group + 1) * WIDE)
                shift = (2 - group) * WIDE
                moved_down = pltpu.roll(ref[part, first, here], LANES - WIDE, 1)
                from_end = pltpu.roll(ref[part, first, end], shift, 1) if shift else ref[part, first, end]
                ref[part, PLANES - 2, here] = jnp.where(
                    lane < 2 * WIDE, moved_down, jnp.where(lane < 3 * WIDE, from_end, ref[part, PLANES - 2, here]))
                to_end = ref[part, last, here]
                to_end = pltpu.roll(to_end, LANES - shift, 1) if shift else to_end
                ref[part, 1, end] = jnp.where(inside, to_end, ref[part, 1, end])

        def across(plane):
            for part in range(2):
                def row(slot, n):
                    return slice(first_row(slot) + n, first_row(slot) + n + 1)

                for j in range(PY):
                    if j > 0:
                        ref[part, plane, row(j, 0)] = ref[part, plane, row(j - 1, CY)]
                    if j < PY - 1:
                        ref[part, plane, row(j, CY + 1)] = ref[part, plane, row(j + 1, 1)]
                top = ref[part, plane, row(4, CY)]
                bottom = ref[part, plane, row(4, 1)]
                extra = ref[part, plane, row(5, 1)]
                lane = lanes_of(top)
                old = ref[part, plane, row(4, 0)]
                ref[part, plane, row(4, 0)] = jnp.where(
                    (lane >= WIDE) & (lane < 3 * WIDE), pltpu.roll(top, WIDE, 1), old)
                old = ref[part, plane, row(4, CY + 1)]
                ref[part, plane, row(4, CY + 1)] = jnp.where(
                    lane < 2 * WIDE, pltpu.roll(bottom, LANES - WIDE, 1),
                    jnp.where(lane < 3 * WIDE, pltpu.roll(extra, 2 * WIDE, 1), old))
                old = ref[part, plane, row(5, 0)]
                ref[part, plane, row(5, 0)] = jnp.where(lane < WIDE, pltpu.roll(top, LANES - 2 * WIDE, 1), old)

        for plane in range(1, PLANES - 1):
            across(plane)

    def mix(self, ref, plane, rows):
        for part in range(2):
            for at in rows:
                below, above = slice(at.start - 1, at.stop - 1), slice(at.start + 1, at.stop + 1)
                mixed = ref[part, plane, below] + ref[part, plane, above] + MIDDLE * ref[part, plane, at]
                self.u_ref[part, plane, at] = (
                    pltpu.roll(mixed, 1, 1) + pltpu.roll(mixed, LANES - 1, 1) + MIDDLE * mixed)

    def smoothed(self, part, plane, at):
        u_ref = self.u_ref
        return u_ref[part, plane - 1, at] + u_ref[part, plane + 1, at] + MIDDLE * u_ref[part, plane, at]

    def sweep(self, ref, first, last, body, rows):
        for plane in range(1, first + 2):
            self.mix(ref, plane, rows)
        for plane in range(first, last + 1):
            body(plane, rows)
            if plane + 2 < PLANES - 1:
                self.mix(ref, plane + 2, rows)

    def precondition(self, ref, right_ref):
        w_ref = self.w_ref
        for part in range(2):
            ref[part, :, 0:BASE] = jnp.zeros((PLANES, BASE, LANES), jnp.float32)
            ref[part, :, ROWS - 8:ROWS] = jnp.zeros((PLANES, 8, LANES), jnp.float32)

        def start(plane):
            for at in tiles():
                r_re, r_im = right_ref[0, plane, at], right_ref[1, plane, at]
                w_re, w_im = w_ref[0, plane, at], w_ref[1, plane, at]
                ref[0, plane, at] = w_re * r_re - w_im * r_im
                ref[1, plane, at] = w_re * r_im + w_im * r_re

        def update(plane, rows):
            for at in rows:
                z_re, z_im = ref[0, plane, at], ref[1, plane, at]
                w_re, w_im = w_ref[0, plane, at], w_ref[1, plane, at]
                g_re = (right_ref[0, plane, at] + self.smoothed(0, plane, at)) - PIVOT * z_re
                g_im = (right_ref[1, plane, at] + self.smoothed(1, plane, at)) - PIVOT * z_im
                ref[0, plane, at] = (1.0 - RELAX) * z_re + (w_re * g_re - w_im * g_im)
                ref[1, plane, at] = (1.0 - RELAX) * z_im + (w_re * g_im + w_im * g_re)

        for plane in range(1, PLANES - 1):
            start(plane)

        @pl.loop(0, SWEEPS - 2)
        def _(number):
            self.sweep(ref, 1, PLANES - 2, update, tiles())

        self.sweep(ref, 2, PLANES - 3, update, own_tiles())
        self.swap_ends(ref)
        self.swap_sides(ref)

    def image(self, ref, out_ref):
        d_ref = self.d_ref

        def body(plane, rows):
            for at in rows:
                z_re, z_im = ref[0, plane, at], ref[1, plane, at]
                d_re, d_im = d_ref[0, plane, at], d_ref[1, plane, at]
                out_ref[0, plane, at] = (d_re * z_re - d_im * z_im) - self.smoothed(0, plane, at)
                out_ref[1, plane, at] = (d_re * z_im + d_im * z_re) - self.smoothed(1, plane, at)

        self.sweep(ref, 2, PLANES - 3, body, own_tiles())


def tiles():
    return [slice(BASE + t * TILE, BASE + (t + 1) * TILE) for t in range(TILES)]


def own_tiles():
    return [slice(first_row(slot) + 1, first_row(slot) + 1 + CY) for slot in range(SLOTS)]


def send_back(ref, back_ref, first):
    for part in range(2):
        for slot in range(SLOTS):
            rows = slice(first_row(slot) + 1, first_row(slot) + 1 + CY)
            turned = ref[part, 2:2 + CX, rows].reshape(LANES, LANES).T
            for unit in range(GROUP):
                if slot_of(unit)[0] == slot:
                    at = slot_of(unit)[1] * WIDE + OWN
                    back_ref[unit, first + part * SLAB:first + (part + 1) * SLAB] = turned[at:at + SLAB]


def solve_kernel(got_ref, below_ref, above_ref, back_ref, sums_ref, r_ref, w_ref, d_ref, q_ref, z_ref, u_ref, turn_ref, turned_ref):
    is_first, is_last = position()
    low_at = jnp.where(is_first, 0, 3)
    high_at = jnp.where(is_last, 30, 27)

    turn_ref[...] = jnp.zeros_like(turn_ref)
    for ref in (r_ref, w_ref, q_ref):
        for plane in range(1, PLANES - 1):
            for part in range(2):
                ref[part, plane, BODY] = jnp.zeros((TILES * TILE, LANES), jnp.float32)

    for unit in range(GROUP):
        slot, group = slot_of(unit)
        at = group * WIDE
        for field in range(FIELDS):
            turn_ref[slot, field, pl.ds(at + low_at, DEEP)] = below_ref[unit, field]
            turn_ref[slot, field, at + OWN:at + OWN + SLAB] = got_ref[unit, field]
            turn_ref[slot, field, pl.ds(at + high_at, DEEP)] = above_ref[unit, field]

    def fix(targets):
        for unit in range(GROUP):
            slot, group = slot_of(unit)
            at = group * WIDE
            for field in range(FIELDS):
                for target, ref, source in targets:
                    if ref is None:
                        row = jnp.zeros((1, LANES), jnp.float32)
                    else:
                        row = ref[unit, field, source:source + 1]
                    turn_ref[slot, field, at + target:at + target + 1] = row

    @pl.when(is_first)
    def _():
        fix(((8, got_ref, 0), (9, None, 0), (10, below_ref, DEEP - 1)))

    @pl.when(is_last)
    def _():
        fix(((27, above_ref, 0), (28, None, 0), (29, got_ref, SLAB - 1)))

    for slot in range(SLOTS):
        for field in range(FIELDS):
            turned_ref[slot, field] = turn_ref[slot, field].T

    def fill(plane, carry):
        at = pl.ds(pl.multiple_of(plane * TILE, TILE), TILE)
        for slot in range(SLOTS):
            b_re, b_im, kappa, damping = [turned_ref[slot, field, at] for field in range(FIELDS)]
            rows = slice(first_row(slot) + 1, first_row(slot) + 1 + CY)
            d_re = CENTER - kappa
            d_im = kappa * damping
            p_re = d_re - MIDDLE
            factor = jnp.where(kappa > 0, (RELAX / SCALE) / (p_re * p_re + d_im * d_im), 0.0)
            r_ref[0, 2 + plane, rows] = SCALE * b_re
            r_ref[1, 2 + plane, rows] = SCALE * b_im
            w_ref[0, 2 + plane, rows] = factor * p_re
            w_ref[1, 2 + plane, rows] = -factor * d_im
            d_ref[0, 2 + plane, rows] = SCALE * d_re
            d_ref[1, 2 + plane, rows] = SCALE * d_im
        return carry

    lax.fori_loop(0, CX, fill, 0, unroll=4)

    steps = Steps(u_ref, w_ref, d_ref)
    steps.swap_sides(r_ref)
    steps.swap_sides(w_ref)
    steps.precondition(z_ref, r_ref)
    send_back(z_ref, back_ref, 0)
    steps.image(z_ref, q_ref)
    steps.swap_ends(q_ref)
    steps.swap_sides(q_ref)
    steps.precondition(z_ref, q_ref)
    send_back(z_ref, back_ref, 2 * SLAB)
    steps.image(z_ref, w_ref)

    lane = lax.broadcasted_iota(jnp.int32, (TILE, LANES), 1)
    place = lax.rem(lane, WIDE)
    in_slab = (place >= OWN) & (place < OWN + SLAB)

    def over_cells(terms, count):
        sums = [jnp.zeros((TILE, LANES), jnp.float32)] * count
        for slot, at in enumerate(own_tiles()):
            here = terms(2, at)
            for plane in range(3, 2 + CX):
                here = [a + b for a, b in zip(here, terms(plane, at))]
            keep = in_slab if slot < SLOTS - 1 else in_slab & (lane < WIDE)
            sums = [a + jnp.where(keep, b, 0.0) for a, b in zip(sums, here)]
        return [total(v) for v in sums]

    def first_terms(plane, at):
        q_re, q_im = q_ref[0, plane, at], q_ref[1, plane, at]
        b_re, b_im = r_ref[0, plane, at], r_ref[1, plane, at]
        t_re, t_im = w_ref[0, plane, at], w_ref[1, plane, at]
        return (q_re * q_re + q_im * q_im, q_re * b_re + q_im * b_im, q_re * b_im - q_im * b_re,
                q_re * t_re + q_im * t_im, q_re * t_im - q_im * t_re)

    norm, proj_re, proj_im, cross_re, cross_im = over_cells(first_terms, 5)
    safe = jnp.where(norm > 0, norm, 1.0)
    cross_re = cross_re / safe
    cross_im = cross_im / safe
    mean_re = jnp.broadcast_to(cross_re, (TILE, LANES))
    mean_im = jnp.broadcast_to(cross_im, (TILE, LANES))

    def second_terms(plane, at):
        q_re, q_im = q_ref[0, plane, at], q_ref[1, plane, at]
        b_re, b_im = r_ref[0, plane, at], r_ref[1, plane, at]
        p_re = w_ref[0, plane, at] - (mean_re * q_re - mean_im * q_im)
        p_im = w_ref[1, plane, at] - (mean_re * q_im + mean_im * q_re)
        return p_re * p_re + p_im * p_im, p_re * b_re + p_im * b_im, p_re * b_im - p_im * b_re

    rest, pair_re, pair_im = over_cells(second_terms, 3)
    row = lax.broadcasted_iota(jnp.int32, (STATS, LANES), 0)
    table = jnp.zeros((STATS, LANES), jnp.float32)
    for n, value in enumerate((norm, proj_re, proj_im, cross_re, cross_im, rest, pair_re, pair_im)):
        table = jnp.where(row == n, value, table)

    for target in range(PZ):
        sums_ref[target] = table


def merged(rows):
    norm, proj_re, proj_im, cross_re, cross_im, rest, pair_re, pair_im = rows

    def over(values):
        return jnp.sum(values, axis=0, keepdims=True)

    whole = over(norm)
    mean_re = over(norm * cross_re) / whole
    mean_im = over(norm * cross_im) / whole
    off_re = cross_re - mean_re
    off_im = cross_im - mean_im
    return (whole, over(proj_re), over(proj_im), mean_re, mean_im,
            over(rest + norm * (off_re * off_re + off_im * off_im)),
            over(pair_re + off_re * proj_re + off_im * proj_im),
            over(pair_im + off_re * proj_im - off_im * proj_re))


def pack_kernel(table_ref, back_ref, out_ref):
    for n, value in enumerate(merged([table_ref[:, n] for n in range(STATS)])):
        for unit in range(GROUP):
            out_ref[unit, FIELDS * SLAB + n:FIELDS * SLAB + n + 1] = value
    for unit in range(GROUP):
        out_ref[unit, 0:FIELDS * SLAB] = back_ref[unit]


def finish_kernel(back_ref, wave_ref, damping_ref, solution_ref, shares_ref):
    rows = [back_ref[:, FIELDS * SLAB + n] for n in range(STATS)]
    norm, proj_re, proj_im, mean_re, mean_im, size, pair_re, pair_im = merged(rows)
    beta_re = pair_re / size
    beta_im = pair_im / size
    lead_re = proj_re / norm - (beta_re * mean_re - beta_im * mean_im)
    lead_im = proj_im / norm - (beta_re * mean_im + beta_im * mean_re)
    shape = (SLAB, LANES)
    beta_re, beta_im, lead_re, lead_im = [jnp.broadcast_to(v, shape) for v in (beta_re, beta_im, lead_re, lead_im)]
    per = LANES // SLAB
    odd, turn = path()
    for tile in range(CZ // LANES):
        pieces = [[], []]
        for source in range(tile * per, (tile + 1) * per):
            at = device_of(source, odd, turn)
            f_re, f_im, s_re, s_im = [back_ref[at, n * SLAB:(n + 1) * SLAB] for n in range(FIELDS)]
            pieces[0].append((lead_re * f_re - lead_im * f_im) + (beta_re * s_re - beta_im * s_im))
            pieces[1].append((lead_re * f_im + lead_im * f_re) + (beta_re * s_im + beta_im * s_re))
        here = slice(tile * LANES, (tile + 1) * LANES)
        x_re, x_im = [jnp.concatenate(p, axis=0).T.reshape(CX, CY, LANES) for p in pieces]
        solution_ref[0, :, :, here] = x_re
        solution_ref[1, :, :, here] = x_im
        u_re, u_im = wave_ref[0, :, :, here], wave_ref[1, :, :, here]
        shares_ref[:, :, here] = (u_re * x_re + u_im * x_im) - damping_ref[:, :, here] * (u_im * x_re - u_re * x_im)


def moved(values, step):
    shots = lax.axis_size("shot")
    pairs = []
    for turn in range(shots):
        chain = []
        for layer in range(PZ):
            odd = layer % 2
            for slab in range(GROUP):
                if slab < RING:
                    device = odd * RING + (turn + 1 + slab) % RING
                else:
                    device = (1 - odd) * RING + (turn - slab) % RING
                chain.append((layer * GROUP + device) * shots + turn)
        pairs += list(zip(chain, chain[1:]) if step > 0 else zip(chain[1:], chain))
    return lax.ppermute(values, ("sub", "shot"), pairs)


def call(kernel, out_shapes, scratch=(), space=pltpu.VMEM, limit=VMEM_LIMIT):
    one = pl.BlockSpec(memory_space=pltpu.VMEM)
    given = pl.BlockSpec(memory_space=space)

    def run(*args):
        return pl.pallas_call(
            kernel,
            out_shape=[jax.ShapeDtypeStruct(shape, jnp.float32) for shape in out_shapes],
            in_specs=[given] * len(args),
            out_specs=[given if space == pltpu.HBM else one] * len(out_shapes),
            scratch_shapes=list(scratch),
            compiler_params=pltpu.CompilerParams(vmem_limit_bytes=limit),
        )(*args)

    return run


def local(adjoint_source, forward_field, kappa, damping):
    source = adjoint_source[0, :, 0]
    wave = forward_field[0, :, 0]
    kappa = kappa[0]
    damping = damping[0]
    block = (CX, CY, CZ)
    held = [pltpu.VMEM(shape, jnp.float32) for shape in ((2,) + block, block, block, (FIELDS, CZ, LANES), (FIELDS, GROUP, SLAB, LANES))]
    message, = call(turn_kernel, [(GROUP, FIELDS, SLAB, LANES)], held + [pltpu.SemaphoreType.DMA((FIELDS,))] * 2,
                    pltpu.HBM, 60 * 1024 * 1024)(source, kappa, damping)
    layers = [[k * GROUP + n for n in range(GROUP)] for k in range(PZ)]
    columns = [[k * GROUP + n for k in range(PZ)] for n in range(GROUP)]
    got = lax.all_to_all(message, "sub", 0, 0, axis_index_groups=layers)
    edge = (GROUP, FIELDS, DEEP, LANES)
    low, high = call(edges_kernel, [edge, edge])(got)
    below = moved(high, 1)
    above = moved(low, -1)
    work = pltpu.VMEM((2, PLANES, ROWS, LANES), jnp.float32)
    turn = pltpu.VMEM((SLOTS, FIELDS, LANES, LANES), jnp.float32)
    back, sums = call(solve_kernel, [(GROUP, FIELDS * SLAB, LANES), (PZ, STATS, LANES)],
                      [work] * 6 + [turn] * 2)(got, below, above)
    table = lax.all_to_all(sums, "sub", 0, 0, axis_index_groups=columns)
    back, = call(pack_kernel, [(GROUP, BACK, LANES)])(table, back)
    back = lax.all_to_all(back, "sub", 0, 0, axis_index_groups=layers)
    solved, shares = call(finish_kernel, [(2, CX, CY, CZ), (CX, CY, CZ)])(back, wave, damping)
    shots = lax.axis_size("shot")
    shares = shares.reshape(shots, CX // shots, CY, CZ)
    share = jnp.sum(lax.all_to_all(shares, "shot", 0, 0), axis=0)
    return (solved[None, :, None], share[None])


def solution(mesh):
    return jax.shard_map(
        local,
        mesh=mesh,
        in_specs=(
            P("shot", None, "sub", None, None, None),
            P("shot", None, "sub", None, None, None),
            P("sub", None, None, None),
            P("sub", None, None, None),
        ),
        out_specs=(P("shot", None, "sub", None, None, None), P("sub", "shot", None, None)),
        check_vma=False,
    )
```
